256 devices in a mesh: dp: 16 (over z_lo, y, core), tensor: 16 (over z_hi, x).
Axes of the slice: x: 4, y: 4, z: 8 (z_hi: 4, z_lo: 2; z = z_hi * 2 + z_lo), core: 2. Of those that a mesh axis runs over, the one named last changes fastest.
Arguments:
- tokens: bfloat16 [131072, 3072], P(('dp', 'tensor')), parts along dimension 0, may hold values from -6 to 6
- expert_ids: int32 [131072, 4], P(('dp', 'tensor')), parts along dimension 0, may hold values from 0 to 15, as said below
- gate_probs: float32 [131072, 4], P(('dp', 'tensor')), parts along dimension 0, may hold values from 0.1 to 1
- gate_weight: bfloat16 [3072, 5376], P(None, 'tensor'), may hold values from -0.109375 to 0.109375
- up_weight: bfloat16 [3072, 5376], P(None, 'tensor'), may hold values from -0.109375 to 0.109375
- down_weight: bfloat16 [5376, 3072], P('tensor'), may hold values from -0.078125 to 0.078125
Outputs:
- mixed: bfloat16 [131072, 3072], P(('dp', 'tensor')), parts along dimension 0
The draws below stay inside these ranges and needn't reach their ends.
There are 16 independent parts, one for each index of `dp`. The reference program is written for one: setup_inputs(seed, part) draws one part's arguments, and reference() takes and returns one part's arrays. A program takes and returns all parts, laid end to end along the dimension named above; an argument that names none is the same for every part. Nothing has to cross between parts.
Inputs may be any that keep to these rules, and one draw needn't show every extreme that they name: `expert_ids`: each row names 4 different experts. In each block of 128 consecutive tokens (rows b * 128 to (b + 1) * 128 - 1) between 1 and 32 rows name expert 0, and some block has exactly 32.
All inputs are finite; a program needn't handle non-finite values.
Results may differ from the reference program's by a relative error of at most 0.019.
Values may be sent and summed in bfloat16 or wider, within the bound.
No kernel may reach another device: no remote copies, remote signals or barrier semaphores. Data moves between devices by JAX's collectives and lax.ppermute only.
A program may use at most 128 MiB of HBM per device.

```python
import jax
import jax.numpy as jnp
from jax import lax

D = 3072
FF = 5376
EXPERTS = 16
TOP = 4
CT = 128
CAP = 32
TOKENS = 8192
N_TENSOR = 16


def draw_expert_ids(key, part):
    key = jax.random.fold_in(key, 11)
    key_list = jax.random.split(key, 5)
    block_count = TOKENS // CT
    counts = jax.random.randint(key_list[0], (block_count,), 1, CAP + 1)
    forced = jax.random.randint(key_list[1], (), 0, block_count)
    counts = jnp.where(jnp.arange(block_count) == forced, CAP, counts)
    scores = jax.random.randint(key_list[2], (block_count, CT), 0, 1 << 20) * CT + jnp.arange(CT)[None, :]
    rank_order = jnp.argsort(jnp.argsort(scores, axis=1), axis=1)
    routed = (rank_order < counts[:, None]).reshape(TOKENS)
    others = jax.random.randint(key_list[3], (TOKENS, EXPERTS - 1), 0, 1 << 20) * EXPERTS + jnp.arange(EXPERTS - 1)[None, :]
    chosen = jnp.argsort(others, axis=1)[:, :TOP] + 1
    position = jax.random.randint(key_list[4], (TOKENS,), 0, TOP)
    window = routed[:, None] & (jnp.arange(TOP)[None, :] == position[:, None])
    return jnp.where(window, 0, chosen).astype(jnp.int32)


def shard_levels(own_key, shape, pieces, low, top_value):
    gain, own = 1.0, jax.random.fold_in(own_key, 6)
    for dim, parts in pieces:
        draws = jnp.exp(jax.random.uniform(jax.random.fold_in(own, dim), (parts,), jnp.float32, low / len(pieces), top_value / len(pieces)))
        gain = gain * jnp.repeat(draws, shape[dim] // parts).reshape([-1 if axis == dim else 1 for axis in range(len(shape))])
    return gain


def scatter_about(rng, shape, width, bound, cuts=(), kind=jnp.bfloat16):
    values = width * jax.random.normal(rng, shape, jnp.float32)
    if cuts:
        values = values * shard_levels(rng, shape, cuts, -0.22, 0.18)
    return jnp.clip(values, -bound, bound).astype(kind)


def setup_inputs(seed: int = 0, part: int = 0) -> dict:
    streams_of = jax.random.split(jax.random.key(seed), 7)
    part_splits = jax.random.split(jax.random.fold_in(streams_of[6], part), 7)
    tokens = scatter_about(part_splits[0], (TOKENS, D), 1.0, 6.0, ((0, 16),))
    expert_ids = draw_expert_ids(jax.random.fold_in(jax.random.fold_in(streams_of[6], part), 71), part)
    gate_probs = jnp.clip(0.1 + 0.9 * jax.random.uniform(part_splits[2], (TOKENS, TOP), jnp.float32) ** shard_levels(part_splits[2], (TOKENS, TOP), ((0, 16),), -0.2, 0.2), 0.1, 1.0)
    gate_weight = scatter_about(streams_of[3], (D, FF), D ** -0.5, 0.109375, ((1, 16),))
    up_weight = scatter_about(streams_of[4], (D, FF), D ** -0.5, 0.109375, ((1, 16),))
    down_weight = scatter_about(streams_of[5], (FF, D), FF ** -0.5, 0.078125, ((0, 16),))
    return dict(tokens=tokens, expert_ids=expert_ids, gate_probs=gate_probs, gate_weight=gate_weight, up_weight=up_weight, down_weight=down_weight)


def reference(tokens, expert_ids, gate_probs, gate_weight, up_weight, down_weight):
    is_window = expert_ids == 0
    routed = jnp.any(is_window, axis=1)
    gate_share = jnp.sum(jnp.where(is_window, gate_probs, 0.0), axis=1)
    block_count = TOKENS // CT
    routed_blocks = routed.reshape(block_count, CT)
    slot_place = jnp.cumsum(routed_blocks.astype(jnp.int32), axis=1).astype(jnp.int32) - 1
    selector = (slot_place[:, None, :] == jnp.arange(CAP, dtype=jnp.int32)[None, :, None]) & routed_blocks[:, None, :]
    slot_rows = jnp.einsum("bst,btd->bsd", selector.astype(jnp.float32), tokens.reshape(block_count, CT, D).astype(jnp.float32))
    slot_rows = slot_rows.astype(jnp.bfloat16).reshape(block_count * CAP, D)
    gate_pre = jnp.dot(slot_rows, gate_weight, preferred_element_type=jnp.float32)
    up_pre = jnp.dot(slot_rows, up_weight, preferred_element_type=jnp.float32)
    hidden = (jax.nn.silu(gate_pre) * up_pre).astype(jnp.bfloat16)
    unit_width = FF // N_TENSOR

    def add_part(part_index, running_sum):
        start_unit = jnp.asarray(part_index).astype(jnp.int32) * unit_width
        columns = lax.dynamic_slice_in_dim(hidden, start_unit, unit_width, 1)
        down_rows = lax.dynamic_slice_in_dim(down_weight, start_unit, unit_width, 0)
        partial_sum = jnp.dot(columns, down_rows, preferred_element_type=jnp.float32).astype(jnp.bfloat16)
        partial_sum = lax.optimization_barrier(partial_sum)
        return running_sum + partial_sum.astype(jnp.float32)

    expert_out = lax.fori_loop(0, N_TENSOR, add_part, jnp.zeros((block_count * CAP, D), jnp.float32))
    slot_index = jnp.where(routed_blocks, jnp.arange(block_count, dtype=jnp.int32)[:, None] * CAP + slot_place, 0)
    picked = jnp.take(expert_out, slot_index.reshape(TOKENS).astype(jnp.int32), axis=0)
    mixed = jnp.where(routed[:, None], gate_share[:, None] * picked, 0.0)
    return mixed.astype(jnp.bfloat16)
```

```python
import jax
import jax.numpy as jnp
import numpy as np
from jax import lax
from jax.sharding import Mesh, PartitionSpec as P

SPANS = 4
CT = 128
CAP = 32
AXES = ("z_lo", "y", "core", "z_hi", "x")
SIZES = (2, 4, 2, 4, 4)
UNITS = 168
SPLIT = 1536
QUARTER = 768


def moved(value, target, sends=lambda z, y, core, x: True):
    pairs = []
    for source in range(int(np.prod(SIZES))):
        z_lo, y, core, z_hi, x = (int(i) for i in np.unravel_index(source, SIZES))
        z = 2 * z_hi + z_lo
        if sends(z, y, core, x):
            z, y, core, x = target(z, y, core, x)
            z, y, core, x = z % 8, y % 4, core % 2, x % 4
            pairs.append((source, int(np.ravel_multi_index((z % 2, y, core, z // 2, x), SIZES))))
    return lax.ppermute(value, AXES, pairs)


def along_z(z, y, core, x):
    return z + 1 - 2 * core, y, core, x


def along_y(z, y, core, x):
    return z, y + 1 - 2 * core, core, x


def other_core(z, y, core, x):
    return z, y, 1 - core, x


def along_x(step):
    return lambda z, y, core, x: (z, y, core, x + step)


def dot_rows(weight, rows):
    return lax.dot_general(weight, rows, (((1,), (1,)), ((), ())), preferred_element_type=jnp.float32)


def on_device(tokens, expert_ids, gate_probs, gate_weight, up_weight, down_weight):
    model_width = tokens.shape[1]
    z_lo, y, core, x = (lax.axis_index(name) for name in ("z_lo", "y", "core", "x"))
    first = z_lo != core
    half = y % 2

    is_window = expert_ids == 0
    routed = jnp.any(is_window, axis=1)
    gate_share = jnp.sum(jnp.where(is_window, gate_probs, 0.0), axis=1)
    routed_blocks = routed.reshape(SPANS, CT)
    slot_place = jnp.cumsum(routed_blocks.astype(jnp.int32), axis=1) - 1
    selector = (
        slot_place[:, None, :] == jnp.arange(CAP, dtype=jnp.int32)[None, :, None]
    ) & routed_blocks[:, None, :]
    slot_rows = jnp.einsum(
        "bst,btd->bsd",
        selector.astype(jnp.bfloat16),
        tokens.reshape(SPANS, CT, model_width),
        preferred_element_type=jnp.float32,
    ).astype(jnp.bfloat16)
    row_piece = lax.all_gather(slot_rows.reshape(SPANS * CAP, model_width), "x", axis=0, tiled=True)
    rows = jnp.concatenate([row_piece, moved(row_piece, other_core)], axis=0)
    rows_here = lax.dynamic_slice_in_dim(rows, half * SPLIT, SPLIT, 1)
    rows_there = lax.dynamic_slice_in_dim(rows, (1 - half) * SPLIT, SPLIT, 1)

    gate_t, up_t = gate_weight.T, up_weight.T
    near, far = core * UNITS, (1 - core) * UNITS

    def piece(array, start, side):
        return lax.dynamic_slice(array, (start, side * SPLIT), (UNITS, SPLIT))

    own = [
        piece(gate_t, near, half),
        piece(up_t, near, half),
        piece(down_weight, near, half),
        piece(gate_t, far, half),
        piece(up_t, far, half),
    ]
    own_down = piece(down_weight, far, half)

    from_z, from_y = [], []
    for step in range(11):
        if step < 5:
            feed = own[step]
        elif step < 7:
            feed = from_z[step - 3]
        elif step < 9:
            lanes = slice((step - 7) * QUARTER, (step - 6) * QUARTER)
            feed = jnp.concatenate([own_down[:, lanes], from_z[4][:, lanes]], axis=1)
        else:
            feed = None
        if step < 2:
            block, sends = feed, lambda z, y, core, x: z % 2 != core
            gets = lambda z, y, core, x: z % 2 == core
        elif feed is None:
            block, sends = from_z[step - 2], lambda z, y, core, x: z % 2 == core
            gets = lambda z, y, core, x: z % 2 != core
        else:
            block, sends = jnp.where(first, feed, from_z[step - 2]), lambda z, y, core, x: True
            gets = sends
        from_z.append(moved(block, along_z, sends))
        from_y.append(moved(from_z[step], along_y, gets))
    here = [jnp.where(first, from_z[i + 2], from_z[i]) for i in range(9)]
    there = [jnp.where(first, from_y[i + 2], from_y[i]) for i in range(9)]

    def hidden(gate_here, gate_there, up_here, up_there):
        gate_pre = dot_rows(gate_here, rows_here) + dot_rows(gate_there, rows_there)
        up_pre = dot_rows(up_here, rows_here) + dot_rows(up_there, rows_there)
        return (jax.nn.silu(gate_pre) * up_pre).astype(jnp.bfloat16)

    hidden_units = jnp.concatenate(
        [
            hidden(own[0], piece(gate_t, near, 1 - half), own[1], piece(up_t, near, 1 - half)),
            hidden(here[0], there[0], here[1], there[1]),
            hidden(here[3], there[3], here[4], there[4]),
            hidden(here[5], there[5], here[6], there[6]),
        ],
        axis=0,
    )

    def outputs(down_own, down_first, last):
        done = []
        for index in range(2):
            lanes = slice(index * QUARTER, (index + 1) * QUARTER)
            parts = [down_own[:, lanes], down_first[:, lanes], last[index][:, :QUARTER], last[index][:, QUARTER:]]
            down = jnp.concatenate(parts, axis=0)
            partial = lax.dot_general(
                hidden_units, down, (((0,), (0,)), ((), ())), preferred_element_type=jnp.float32
            )
            mine, others = partial[:512], partial[512:].astype(jnp.bfloat16)
            sums = mine + moved(others, other_core).astype(jnp.float32)
            sums = sums.astype(jnp.bfloat16).reshape(4, SPANS * CAP, QUARTER)
            total = lax.dynamic_index_in_dim(sums, x, 0, False).astype(jnp.float32)
            for step in (1, 3, 2):
                sent = lax.dynamic_index_in_dim(sums, (x + step) % 4, 0, False)
                total = total + moved(sent, along_x(step)).astype(jnp.float32)
            done.append(total)
        return jnp.concatenate(done, axis=1)

    out_here = outputs(own[2], here[2], here[7:9])
    out_there = outputs(piece(down_weight, near, 1 - half), there[2], there[7:9])
    low = half == 0
    expert_out = jnp.concatenate(
        [jnp.where(low, out_here, out_there), jnp.where(low, out_there, out_here)], axis=1
    ).reshape(SPANS, CAP, model_width)
    high_part = expert_out.astype(jnp.bfloat16)
    low_part = (expert_out - high_part.astype(jnp.float32)).astype(jnp.bfloat16)
    places = selector.astype(jnp.bfloat16)
    picked = jnp.einsum("bst,bsd->btd", places, high_part, preferred_element_type=jnp.float32)
    picked = picked + jnp.einsum("bst,bsd->btd", places, low_part, preferred_element_type=jnp.float32)
    mixed = gate_share[:, None] * picked.reshape(SPANS * CT, model_width)
    return mixed.astype(jnp.bfloat16)


def solution(mesh):
    grid = Mesh(mesh.devices.reshape(SIZES), AXES)
    shard = ("z_hi", "x")
    in_specs = (
        P(AXES, None),
        P(AXES, None),
        P(AXES, None),
        P(None, shard),
        P(None, shard),
        P(shard, None),
    )
    return jax.shard_map(
        on_device, mesh=grid, in_specs=in_specs, out_specs=P(AXES, None), check_vma=False
    )
```

```python
import jax
import jax.numpy as jnp
import numpy as np
from jax import lax
from jax.sharding import Mesh, PartitionSpec as P

SPANS = 4
CT = 128
CAP = 32
AXES = ("z_lo", "y", "core", "z_hi", "x")
SIZES = (2, 4, 2, 4, 4)
UNITS = 168
SPLIT = 1536
QUARTER = 768


def moved(value, target, sends=None):
    pairs = []
    for source in range(int(np.prod(SIZES))):
        z_lo, y, core, z_hi, x = (int(i) for i in np.unravel_index(source, SIZES))
        z = 2 * z_hi + z_lo
        if sends is None or sends(z, y, core, x):
            z, y, core, x = target(z, y, core, x)
            z, y, core, x = z % 8, y % 4, core % 2, x % 4
            pairs.append((source, int(np.ravel_multi_index((z % 2, y, core, z // 2, x), SIZES))))
    return lax.ppermute(value, AXES, pairs)


def is_second(wanted):
    return lambda z, y, core, x: (z % 2 == core) == wanted


def along_z(z, y, core, x):
    return z + 1 - 2 * core, y, core, x


def along_y(z, y, core, x):
    return z, y + 1 - 2 * core, core, x


def other_core(z, y, core, x):
    return z, y, 1 - core, x


def along_x(step):
    return lambda z, y, core, x: (z, y, core, x + step)


def dot_rows(weight, rows):
    return lax.dot_general(weight, rows, (((1,), (1,)), ((), ())), preferred_element_type=jnp.float32)


def on_device(tokens, expert_ids, gate_probs, gate_weight, up_weight, down_weight):
    model_width = tokens.shape[1]
    z_lo, y, core, x = (lax.axis_index(name) for name in ("z_lo", "y", "core", "x"))
    first = z_lo != core
    half = y % 2

    is_window = expert_ids == 0
    routed = jnp.any(is_window, axis=1)
    gate_share = jnp.sum(jnp.where(is_window, gate_probs, 0.0), axis=1)
    routed_blocks = routed.reshape(SPANS, CT)
    slot_place = jnp.cumsum(routed_blocks.astype(jnp.int32), axis=1) - 1
    selector = (
        slot_place[:, None, :] == jnp.arange(CAP, dtype=jnp.int32)[None, :, None]
    ) & routed_blocks[:, None, :]
    slot_rows = jnp.einsum(
        "bst,btd->bsd",
        selector.astype(jnp.bfloat16),
        tokens.reshape(SPANS, CT, model_width),
        preferred_element_type=jnp.float32,
    ).astype(jnp.bfloat16)
    near, far = core * UNITS, (1 - core) * UNITS

    def piece(array, start, side):
        return lax.dynamic_slice(array, (start, side * SPLIT), (UNITS, SPLIT))

    shard = [gate_weight.T, up_weight.T, down_weight]
    order = [(0, near), (1, near), (2, near), (0, far), (1, far), (2, far)]
    own = [piece(shard[0], near, half)]
    def taken(parts, index):
        return jnp.where(first, parts[index + 2], parts[index])

    def both(side_rows, here_parts, there_parts):
        here_part, there_part = (jnp.concatenate(parts, axis=0) for parts in (here_parts, there_parts))
        return dot_rows(side_rows[0], here_part) + dot_rows(side_rows[1], there_part)

    def gated(gate_pre, up_pre):
        return (jax.nn.silu(gate_pre) * up_pre).astype(jnp.bfloat16)

    from_z, from_y = [], []
    rows, work = None, None
    for step in range(13):
        if step < 5:
            feed = own[step]
        elif step < 7:
            feed = from_z[step - 3]
        elif step < 9:
            lanes = slice((step - 7) * QUARTER, (step - 6) * QUARTER)
            feed = jnp.concatenate([own[5][:, lanes], from_z[4][:, lanes]], axis=1)
        if step < 2:
            block, sends, gets = feed, is_second(False), is_second(True)
        elif step < 9:
            block, sends, gets = jnp.where(first, feed, from_z[step - 2]), None, None
        else:
            block, sends, gets = from_z[step - 2], is_second(True), is_second(False)
        landed = max(step - 1, 0)
        settled = from_y[max(step - 4, 0) : max(step - 3, 0)]
        if step == 1:
            work = slot_rows
        if step == 8:
            work = rows
        block, from_z[:landed], settled, own, shard, work = lax.optimization_barrier(
            (block, from_z[:landed], settled, own, shard, work)
        )
        if step >= 4:
            from_y[step - 4] = settled[0]
        if step < 5:
            own.append(piece(shard[order[step + 1][0]], order[step + 1][1], half))
        if step < 11:
            from_z.append(moved(block, along_z, sends))
        if step >= 2:
            from_y.append(moved(from_z[step - 2], along_y, is_second(True) if step < 4 else None if step < 11 else is_second(False)))
        if step == 1:
            rows = lax.all_gather(work.reshape(SPANS * CAP, model_width), ("core", "x"), axis=0, tiled=True)
            work = None
        if step == 8:
            side_rows = [lax.dynamic_slice_in_dim(work, side * SPLIT, SPLIT, 1) for side in (half, 1 - half)]
            rest = [piece(array, near, 1 - half) for array in shard]
            gate_pre = both(side_rows, [own[0], taken(from_z, 0)], [rest[0], taken(from_y, 0)])
            work = (side_rows, rest, gate_pre)
        if step == 9:
            side_rows, rest, gate_pre = work
            up_pre = both(side_rows, [own[1], taken(from_z, 1)], [rest[1], taken(from_y, 1)])
            work = (side_rows, rest, [gated(gate_pre, up_pre)])
        if step == 10:
            side_rows, rest, hidden = work
            gate_pre = both(side_rows, [taken(from_z, 3)], [taken(from_y, 3)])
            up_pre = both(side_rows, [taken(from_z, 4)], [taken(from_y, 4)])
            work = (side_rows, rest, hidden + [gated(gate_pre, up_pre)])
        if step == 11:
            side_rows, rest, hidden = work
            pre = [dot_rows(side_rows[0], taken(from_z, i)) for i in (5, 6)]
            work = (side_rows, rest, hidden, pre)
        if step == 12:
            side_rows, rest, hidden, pre = work
            pre = [pre[i] + dot_rows(side_rows[1], taken(from_y, 5 + i)) for i in (0, 1)]
            hidden_units = jnp.concatenate(hidden + [gated(*pre)], axis=1)

    def outputs(down_own, down_first, last):
        done = []
        for index in range(2):
            lanes = slice(index * QUARTER, (index + 1) * QUARTER)
            parts = [down_own[:, lanes], down_first[:, lanes], last[index][:, :QUARTER], last[index][:, QUARTER:]]
            down = jnp.concatenate(parts, axis=0)
            partial = jnp.dot(hidden_units, down, preferred_element_type=jnp.float32)
            mine = lax.dynamic_slice_in_dim(partial, core * 512, 512, 0)
            others = lax.dynamic_slice_in_dim(partial, (1 - core) * 512, 512, 0).astype(jnp.bfloat16)
            sums = mine + moved(others, other_core).astype(jnp.float32)
            sums = sums.astype(jnp.bfloat16).reshape(4, SPANS * CAP, QUARTER)
            total = lax.dynamic_index_in_dim(sums, x, 0, False).astype(jnp.float32)
            for step in (1, 3, 2):
                sent = lax.dynamic_index_in_dim(sums, (x + step) % 4, 0, False)
                total = total + moved(sent, along_x(step)).astype(jnp.float32)
            done.append(total)
        return jnp.concatenate(done, axis=1)

    out_here = outputs(own[2], taken(from_z, 2), [taken(from_z, i) for i in (7, 8)])
    out_there = outputs(rest[2], taken(from_y, 2), [taken(from_y, i) for i in (7, 8)])
    low = half == 0
    expert_out = jnp.concatenate(
        [jnp.where(low, out_here, out_there), jnp.where(low, out_there, out_here)], axis=1
    ).reshape(SPANS, CAP, model_width)
    high_part = expert_out.astype(jnp.bfloat16)
    low_part = (expert_out - high_part.astype(jnp.float32)).astype(jnp.bfloat16)
    places = selector.astype(jnp.bfloat16)
    picked = jnp.einsum("bst,bsd->btd", places, high_part, preferred_element_type=jnp.float32)
    picked = picked + jnp.einsum("bst,bsd->btd", places, low_part, preferred_element_type=jnp.float32)
    mixed = gate_share[:, None] * picked.reshape(SPANS * CT, model_width)
    return mixed.astype(jnp.bfloat16)


def solution(mesh):
    grid = Mesh(mesh.devices.reshape(SIZES), AXES)
    shard = ("z_hi", "x")
    in_specs = (
        P(AXES, None),
        P(AXES, None),
        P(AXES, None),
        P(None, shard),
        P(None, shard),
        P(shard, None),
    )
    return jax.shard_map(
        on_device, mesh=grid, in_specs=in_specs, out_specs=P(AXES, None), check_vma=False
    )
```

```python
import functools

import jax
import jax.numpy as jnp
import numpy as np
from jax import lax
from jax.experimental import pallas as pl
from jax.experimental.pallas import tpu as pltpu
from jax.sharding import Mesh, PartitionSpec as P

SPANS = 4
CT = 128
CAP = 32
AXES = ("z_lo", "y", "core", "z_hi", "x")
SIZES = (2, 4, 2, 4, 4)
UNITS = 168
SPLIT = 1536
ROWS = 512
ALL_VMEM_BYTES = 60 * 1024 * 1024


def moved(value, target, sends=None):
    pairs = []
    for source in range(int(np.prod(SIZES))):
        z_lo, y, core, z_hi, x = (int(i) for i in np.unravel_index(source, SIZES))
        z = 2 * z_hi + z_lo
        if sends is None or sends(z, y, core, x):
            z, y, core, x = target(z, y, core, x)
            z, y, core, x = z % 8, y % 4, core % 2, x % 4
            pairs.append((source, int(np.ravel_multi_index((z % 2, y, core, z // 2, x), SIZES))))
    return lax.ppermute(value, AXES, pairs)


def is_second(wanted):
    return lambda z, y, core, x: (z % 2 == core) == wanted


def along_z(z, y, core, x):
    return z + 1 - 2 * core, y, core, x


def along_y(z, y, core, x):
    return z, y + 1 - 2 * core, core, x


def other_core(z, y, core, x):
    return z, y, 1 - core, x


def along_x(step):
    return lambda z, y, core, x: (z, y, core, x + step)


def grouped(refs, counts):
    refs = list(refs)
    return [[refs.pop(0) for _ in range(count)] for count in counts]


class Staged:
    def __init__(self, place_ref, sources, staged, sems):
        self.sources, self.staged, self.sems = sources, staged, sems
        feeds = place_ref[0] == 1
        for option in (0, 1):

            @pl.when(feeds == (option == 1))
            def _(option=option):
                for index in range(len(sources)):
                    self.copy(index, option).start()

    def copy(self, index, option):
        options = self.sources[index]
        option = min(option, len(options) - 1)
        return pltpu.make_async_copy(options[option], self.staged.at[index], self.sems.at[index])

    def keep_units(self, place_ref, kept, owned=0):
        here = pl.multiple_of(place_ref[2] * SPLIT, SPLIT)
        lanes = [pl.ds(here, SPLIT), pl.ds(SPLIT - here, SPLIT)]
        for index in range(len(self.sources)):
            self.copy(index, 0).wait()
            start = (owned + index // 4) * UNITS
            kept[index // 2 % 2][start : start + UNITS, lanes[index % 2]] = self.staged[index]

    def keep_down(self, kept):
        for index in range(len(self.sources)):
            self.copy(index, 0).wait()
            kept[index * UNITS : (index + 1) * UNITS, :] = self.staged[index]


SPANS_OF_ROWS = [pl.ds(start, ROWS) for start in range(0, 2 * ROWS, ROWS)]


def row_copies(rows_ref, rows_kept, sems):
    return [
        pltpu.make_async_copy(rows_ref.at[span], rows_kept.at[span], sems.at[index])
        for index, span in enumerate(SPANS_OF_ROWS)
    ]


def hidden_of(rows, gate_kept, up_kept):
    gate_pre, up_pre = (
        lax.dot_general(rows, kept[...], (((1,), (1,)), ((), ())), preferred_element_type=jnp.float32)
        for kept in (gate_kept, up_kept)
    )
    return (gate_pre / (1.0 + jnp.exp(-gate_pre)) * up_pre).astype(jnp.bfloat16)


def early_kernel(counts, place_ref, rows_ref, *refs):
    total = sum(counts)
    own_ref, out_ref, rows_kept, own_kept, staged, gate_kept, up_kept, sems, row_sems = refs[total:]
    blocks = Staged(place_ref, grouped(refs[:total], counts), staged, sems)
    copies = row_copies(rows_ref, rows_kept, row_sems)
    for copy in copies:
        copy.start()
    own_copy = pltpu.make_async_copy(own_ref, own_kept, row_sems.at[2])
    own_copy.start()
    blocks.keep_units(place_ref, (gate_kept, up_kept), owned=1)
    own_copy.wait()
    gate_kept[:UNITS, :] = own_kept[:UNITS, :]
    up_kept[:UNITS, :] = own_kept[UNITS:, :]
    for copy, span in zip(copies, SPANS_OF_ROWS):
        copy.wait()
        out_ref[span, :] = hidden_of(rows_kept[span, :], gate_kept, up_kept)


def down_into(place_ref, outs, first, last, kept):
    core = place_ref[1]
    for owner, out_ref in zip((1 - core, core), outs):
        span = pl.ds(pl.multiple_of(owner * ROWS, ROWS), ROWS)
        units = jnp.concatenate([first[span, :], last[span, :]], axis=1)
        out_ref[...] = jnp.dot(units, kept[...], preferred_element_type=jnp.float32).astype(jnp.bfloat16)


def late_kernel(unit_counts, down_counts, place_ref, rows_ref, first_ref, *refs):
    split = sum(unit_counts)
    total = split + sum(down_counts)
    others_ref, mine_ref, last_ref = refs[total : total + 3]
    rows_kept, first_kept, staged, gate_kept, up_kept, down_kept, sems, row_sems = refs[total + 3 :]
    units = len(unit_counts)
    blocks = Staged(place_ref, grouped(refs[:split], unit_counts), staged.at[pl.ds(0, units)], sems.at[pl.ds(0, units)])
    copies = row_copies(rows_ref, rows_kept, row_sems)
    for copy in copies:
        copy.start()
    downs = Staged(
        place_ref, grouped(refs[split:total], down_counts), staged.at[pl.ds(units, 4)], sems.at[pl.ds(units, 4)]
    )
    first_copy = pltpu.make_async_copy(first_ref, first_kept, row_sems.at[2])
    first_copy.start()
    blocks.keep_units(place_ref, (gate_kept, up_kept))
    for copy, span in zip(copies, SPANS_OF_ROWS):
        copy.wait()
        last_ref[span, :] = hidden_of(rows_kept[span, :], gate_kept, up_kept)
    downs.keep_down(down_kept)
    first_copy.wait()
    down_into(place_ref, (others_ref, mine_ref), first_kept, last_ref, down_kept)


def down_kernel(down_counts, place_ref, first_ref, last_ref, *refs):
    total = sum(down_counts)
    others_ref, mine_ref, first_kept, last_kept, staged, down_kept, sems, row_sems = refs[total:]
    downs = Staged(place_ref, grouped(refs[:total], down_counts), staged, sems)
    copies = [
        pltpu.make_async_copy(first_ref, first_kept, row_sems.at[0]),
        pltpu.make_async_copy(last_ref, last_kept, row_sems.at[1]),
    ]
    for copy in copies:
        copy.start()
    downs.keep_down(down_kept)
    for copy in copies:
        copy.wait()
    down_into(place_ref, (others_ref, mine_ref), first_kept, last_kept, down_kept)


def whole(*shape):
    return pl.BlockSpec(shape, lambda: (0,) * len(shape))


def kernel_call(kernel, place, arrays, outs, scratch):
    return pl.pallas_call(
        kernel,
        out_shape=[jax.ShapeDtypeStruct(shape, jnp.bfloat16) for shape in outs],
        in_specs=[pl.BlockSpec(memory_space=pltpu.SMEM)]
        + [pl.BlockSpec(memory_space=pltpu.HBM)] * len(arrays),
        out_specs=[whole(*shape) for shape in outs],
        scratch_shapes=scratch,
        compiler_params=pltpu.CompilerParams(vmem_limit_bytes=ALL_VMEM_BYTES),
        cost_estimate=pl.CostEstimate(flops=1000000, bytes_accessed=100000, transcendentals=0),
    )(place, *arrays)


def vmem(*shape):
    return pltpu.VMEM(shape, jnp.bfloat16)


def flat(sources):
    return [array for source in sources for array in source]


def early_hidden(place, rows, sources, own):
    units = (1 + len(sources) // 4) * UNITS
    scratch = [
        vmem(2 * ROWS, 2 * SPLIT),
        vmem(*own.shape),
        vmem(len(sources), UNITS, SPLIT),
        vmem(units, 2 * SPLIT),
        vmem(units, 2 * SPLIT),
        pltpu.SemaphoreType.DMA((len(sources),)),
        pltpu.SemaphoreType.DMA((3,)),
    ]
    kernel = functools.partial(early_kernel, [len(source) for source in sources])
    return kernel_call(kernel, place, [rows, *flat(sources), own], [(2 * ROWS, units)], scratch)[0]


def late_products(place, rows, first, sources, down_sources):
    scratch = [
        vmem(2 * ROWS, 2 * SPLIT),
        vmem(*first.shape),
        vmem(8, UNITS, SPLIT),
        vmem(UNITS, 2 * SPLIT),
        vmem(UNITS, 2 * SPLIT),
        vmem(4 * UNITS, SPLIT),
        pltpu.SemaphoreType.DMA((8,)),
        pltpu.SemaphoreType.DMA((3,)),
    ]
    kernel = functools.partial(late_kernel, [len(source) for source in sources], [len(source) for source in down_sources])
    arrays = [rows, first, *flat(sources), *flat(down_sources)]
    return kernel_call(kernel, place, arrays, [(ROWS, SPLIT), (ROWS, SPLIT), (2 * ROWS, UNITS)], scratch)


def down_products(place, first, last, down_sources):
    scratch = [
        vmem(*first.shape),
        vmem(*last.shape),
        vmem(4, UNITS, SPLIT),
        vmem(4 * UNITS, SPLIT),
        pltpu.SemaphoreType.DMA((4,)),
        pltpu.SemaphoreType.DMA((2,)),
    ]
    kernel = functools.partial(down_kernel, [len(source) for source in down_sources])
    return kernel_call(kernel, place, [first, last, *flat(down_sources)], [(ROWS, SPLIT)] * 2, scratch)


def spread_kernel(place_ref, places_ref, share_ref, *refs):
    out_ref = refs[-1]
    here = pl.multiple_of(place_ref[2] * SPLIT, SPLIT)
    places = places_ref[...]
    for index, lanes in enumerate((pl.ds(here, SPLIT), pl.ds(SPLIT - here, SPLIT))):
        if index == 0:
            parts = [refs[0][...]]
        else:
            expert_out = refs[1][...] + refs[2][...].astype(jnp.float32) + refs[3][...].astype(jnp.float32)
            high = expert_out.astype(jnp.bfloat16)
            parts = [high, (expert_out - high.astype(jnp.float32)).astype(jnp.bfloat16)]
        picked = [jnp.dot(places, part, preferred_element_type=jnp.float32) for part in parts]
        out_ref[:, lanes] = (share_ref[...] * sum(picked[1:], picked[0])).astype(jnp.bfloat16)


def spread(place, places, share, terms):
    block = lambda shape: pl.BlockSpec(shape, lambda i, place: (i, 0))
    return pl.pallas_call(
        spread_kernel,
        out_shape=jax.ShapeDtypeStruct((SPANS * CT, 2 * SPLIT), jnp.bfloat16),
        grid_spec=pltpu.PrefetchScalarGridSpec(
            num_scalar_prefetch=1,
            grid=(SPANS,),
            in_specs=[block((CT, CAP)), block((CT, 1))] + [block((CAP, term.shape[1])) for term in terms],
            out_specs=block((CT, 2 * SPLIT)),
        ),
        compiler_params=pltpu.CompilerParams(vmem_limit_bytes=ALL_VMEM_BYTES),
    )(place, places, share, *terms)


def on_device(tokens, expert_ids, gate_probs, gate_weight, up_weight, down_weight):
    model_width = tokens.shape[1]
    z_lo, y, core, x = (lax.axis_index(name) for name in ("z_lo", "y", "core", "x"))
    first = z_lo != core
    half = y % 2

    is_window = expert_ids == 0
    routed = jnp.any(is_window, axis=1)
    gate_share = jnp.sum(jnp.where(is_window, gate_probs, 0.0), axis=1)
    routed_blocks = routed.reshape(SPANS, CT)
    slot_place = jnp.cumsum(routed_blocks.astype(jnp.int32), axis=1) - 1
    selector = (
        slot_place[:, None, :] == jnp.arange(CAP, dtype=jnp.int32)[None, :, None]
    ) & routed_blocks[:, None, :]
    slot_rows = jnp.einsum(
        "bst,btd->bsd",
        selector.astype(jnp.bfloat16),
        tokens.reshape(SPANS, CT, model_width),
        preferred_element_type=jnp.float32,
    ).astype(jnp.bfloat16).reshape(SPANS * CAP, model_width)
    near_units, far_units = core * UNITS, (1 - core) * UNITS

    def piece(array, start, side):
        return lax.dynamic_slice(array, (start, side * SPLIT), (UNITS, SPLIT))

    shard = [gate_weight.T, up_weight.T, down_weight]
    order = [(0, near_units), (1, near_units), (2, near_units), (0, far_units), (1, far_units), (2, far_units)]
    own = [piece(shard[0], near_units, half)]
    place = jnp.stack([first.astype(jnp.int32), core, half])

    def joined(*parts):
        return jnp.concatenate(parts, axis=0)

    def pick(parts, index):
        return (parts[index], parts[index + 2])

    from_z, from_y = [], []
    work = slot_rows
    for step in range(13):
        if step < 5:
            feed = own[step]
        elif step < 7:
            feed = from_z[step - 3]
        elif step < 9:
            feed = own[5] if step == 7 else from_z[4]
        if step < 2:
            block, sends = feed, is_second(False)
        elif step < 9:
            block, sends = jnp.where(first, feed, from_z[step - 2]), None
        else:
            block, sends = from_z[step - 2], is_second(True)
        landed = max(step - 1, 0)
        settled = from_y[max(step - 4, 0) : max(step - 3, 0)]
        if step == 8:
            work["rows"] = rows
        block, from_z[:landed], settled, own, shard, work = lax.optimization_barrier(
            (block, from_z[:landed], settled, own, shard, work)
        )
        if step >= 4:
            from_y[step - 4] = settled[0]
        if step < 5:
            own.append(piece(shard[order[step + 1][0]], order[step + 1][1], half))
        if step < 11:
            from_z.append(moved(block, along_z, sends))
        if step >= 2:
            gets = is_second(True) if step < 4 else None if step < 11 else is_second(False)
            from_y.append(moved(from_z[step - 2], along_y, gets))
        if step == 0:
            rows = lax.all_gather(work, ("core", "x"), axis=0, tiled=True)
            work = {}
        if step == 8:
            own_parts = [lax.dynamic_slice_in_dim(array, near_units, UNITS, 0) for array in shard[:2]]
            work["own"] = joined(*own_parts[:2])
            work["down"] = [piece(shard[2], near_units, side) for side in (half, 1 - half)]
        def block_at(index):
            return [pick(from_z, index), pick(from_y, index), pick(from_z, index + 1), pick(from_y, index + 1)]

        if step == 10:
            work["hidden"] = early_hidden(place, work["rows"], block_at(0) + block_at(3), work["own"])

    def downs(side, parts):
        return [(work["down"][side],), pick(parts, 2), pick(parts, 7), pick(parts, 8)]

    others_here, mine_here, last = late_products(place, work["rows"], work["hidden"], block_at(5), downs(0, from_z))
    others_here, last, from_y[9], from_y[10] = lax.optimization_barrier((others_here, last, from_y[9], from_y[10]))
    sums_here = (mine_here.astype(jnp.float32) + moved(others_here, other_core).astype(jnp.float32)).astype(jnp.bfloat16)
    out_here = lax.psum_scatter(sums_here, "x", scatter_dimension=0, tiled=True)
    others_there, mine_there = down_products(place, work["hidden"], last, downs(1, from_y))
    pair_there = (mine_there, moved(others_there, other_core))

    def summed(pair, step):
        start = (x + step) % 4 * (SPANS * CAP)
        first_part, second_part = (lax.dynamic_slice_in_dim(part, start, SPANS * CAP, 0) for part in pair)
        return first_part.astype(jnp.float32) + second_part.astype(jnp.float32)

    half_rows = SPANS * CAP // 2

    def far_pieces(pair):
        piece_on = summed(pair, 2).astype(jnp.bfloat16)
        return piece_on[:half_rows], piece_on[half_rows:]

    def far(pieces):
        return moved(pieces[0], along_x(1)), moved(pieces[1], along_x(3))

    def near(pair, arrived):
        above, below = summed(pair, 1), summed(pair, 3)
        above = joined(above[:half_rows] + arrived[0].astype(jnp.float32), above[half_rows:]).astype(jnp.bfloat16)
        below = joined(below[:half_rows], below[half_rows:] + arrived[1].astype(jnp.float32)).astype(jnp.bfloat16)
        return [moved(above, along_x(1)), moved(below, along_x(3))]

    pieces_there, pair_there = lax.optimization_barrier((far_pieces(pair_there), pair_there))
    near_there = near(pair_there, far(pieces_there))
    terms = [out_here, summed(pair_there, 0), *near_there]
    places = jnp.swapaxes(selector, 1, 2).reshape(SPANS * CT, CAP).astype(jnp.bfloat16)
    return spread(place, places, gate_share[:, None], terms)


def solution(mesh):
    grid = Mesh(mesh.devices.reshape(SIZES), AXES)
    shard = ("z_hi", "x")
    in_specs = (
        P(AXES, None),
        P(AXES, None),
        P(AXES, None),
        P(None, shard),
        P(None, shard),
        P(shard, None),
    )
    return jax.shard_map(
        on_device, mesh=grid, in_specs=in_specs, out_specs=P(AXES, None), check_vma=False
    )
```

```python
import functools

import jax
import jax.numpy as jnp
import numpy as np
from jax import lax
from jax.experimental import pallas as pl
from jax.experimental.pallas import tpu as pltpu
from jax.sharding import Mesh, PartitionSpec as P

SPANS = 4
CT = 128
CAP = 32
AXES = ("z_lo", "y", "core", "z_hi", "x")
SIZES = (2, 4, 2, 4, 4)
UNITS = 168
SPLIT = 1536
ROWS = 512
ALL_VMEM_BYTES = 60 * 1024 * 1024


def moved(value, target):
    pairs = []
    for source in range(int(np.prod(SIZES))):
        z_lo, y, core, z_hi, x = (int(i) for i in np.unravel_index(source, SIZES))
        z = 2 * z_hi + z_lo
        z, y, core, x = target(z, y, core, x)
        z, y, core, x = z % 8, y % 4, core % 2, x % 4
        pairs.append((source, int(np.ravel_multi_index((z % 2, y, core, z // 2, x), SIZES))))
    return lax.ppermute(value, AXES, pairs)


def along_z(z, y, core, x):
    return z + 1 - 2 * core, y, core, x


def along_y(z, y, core, x):
    return z, y + 1 - 2 * core, core, x


def other_core(z, y, core, x):
    return z, y, 1 - core, x


def along_x(step):
    return lambda z, y, core, x: (z, y, core, x + step)


def grouped(refs, counts):
    refs = list(refs)
    return [[refs.pop(0) for _ in range(count)] for count in counts]


class Staged:
    def __init__(self, place_ref, sources, staged, sems):
        self.sources, self.staged, self.sems = sources, staged, sems
        feeds = place_ref[0] == 1
        for option in (0, 1):

            @pl.when(feeds == (option == 1))
            def _(option=option):
                for index in range(len(sources)):
                    self.copy(index, option).start()

    def copy(self, index, option):
        options = self.sources[index]
        option = min(option, len(options) - 1)
        return pltpu.make_async_copy(options[option], self.staged.at[index], self.sems.at[index])

    def keep_units(self, place_ref, kept, owned=0):
        here = pl.multiple_of(place_ref[2] * SPLIT, SPLIT)
        lanes = [pl.ds(here, SPLIT), pl.ds(SPLIT - here, SPLIT)]
        for index in range(len(self.sources)):
            self.copy(index, 0).wait()
            start = (owned + index // 4) * UNITS
            kept[index // 2 % 2][start : start + UNITS, lanes[index % 2]] = self.staged[index]

    def keep_down(self, kept):
        for index in range(len(self.sources)):
            self.copy(index, 0).wait()
            kept[index * UNITS : (index + 1) * UNITS, :] = self.staged[index]


SPANS_OF_ROWS = [pl.ds(start, ROWS) for start in range(0, 2 * ROWS, ROWS)]


def row_copies(rows_ref, rows_kept, sems):
    return [
        pltpu.make_async_copy(rows_ref.at[span], rows_kept.at[span], sems.at[index])
        for index, span in enumerate(SPANS_OF_ROWS)
    ]


def hidden_rows(copies, rows_kept, gate_kept, up_kept, out_ref):
    for copy in copies:
        copy.wait()

    @pl.loop(0, 2 * ROWS, step=ROWS)
    def _(start):
        span = pl.ds(pl.multiple_of(start, ROWS), ROWS)
        gate_pre, up_pre = (
            lax.dot_general(
                rows_kept[span, :], kept[...], (((1,), (1,)), ((), ())), preferred_element_type=jnp.float32
            )
            for kept in (gate_kept, up_kept)
        )
        out_ref[span, :] = (gate_pre / (1.0 + jnp.exp(-gate_pre)) * up_pre).astype(jnp.bfloat16)


def early_kernel(counts, place_ref, rows_ref, *refs):
    total = sum(counts)
    own_refs, (out_ref, rows_kept, own_kept, staged, gate_kept, up_kept, sems, row_sems) = refs[total : total + 2], refs[total + 2 :]
    own_copies = [
        pltpu.make_async_copy(own_refs[index], own_kept.at[index], row_sems.at[2 + index]) for index in (0, 1)
    ]
    for copy in own_copies:
        copy.start()
    blocks = Staged(place_ref, grouped(refs[:total], counts), staged, sems)
    copies = row_copies(rows_ref, rows_kept, row_sems)
    for copy in copies:
        copy.start()
    for index, kept in enumerate((gate_kept, up_kept)):
        own_copies[index].wait()
        kept[:UNITS, :] = own_kept[index]
    blocks.keep_units(place_ref, (gate_kept, up_kept), owned=1)
    hidden_rows(copies, rows_kept, gate_kept, up_kept, out_ref)


def down_into(place_ref, outs, first, last, kept):
    core = place_ref[1]
    for owner, out_ref in zip((1 - core, core), outs):
        span = pl.ds(pl.multiple_of(owner * ROWS, ROWS), ROWS)
        units = jnp.concatenate([first[span, :], last[span, :]], axis=1)
        out_ref[...] = jnp.dot(units, kept[...], preferred_element_type=jnp.float32).astype(jnp.bfloat16)


def late_kernel(unit_counts, down_counts, place_ref, rows_ref, first_ref, *refs):
    split = sum(unit_counts)
    total = split + sum(down_counts)
    others_ref, mine_ref, last_ref = refs[total : total + 3]
    rows_kept, first_kept, staged, gate_kept, up_kept, down_kept, sems, row_sems = refs[total + 3 :]
    units = len(unit_counts)
    blocks = Staged(place_ref, grouped(refs[:split], unit_counts), staged.at[pl.ds(0, units)], sems.at[pl.ds(0, units)])
    copies = row_copies(rows_ref, rows_kept, row_sems)
    for copy in copies:
        copy.start()
    downs = Staged(
        place_ref, grouped(refs[split:total], down_counts), staged.at[pl.ds(units, 4)], sems.at[pl.ds(units, 4)]
    )
    first_copy = pltpu.make_async_copy(first_ref, first_kept, row_sems.at[2])
    first_copy.start()
    blocks.keep_units(place_ref, (gate_kept, up_kept))
    hidden_rows(copies, rows_kept, gate_kept, up_kept, last_ref)
    downs.keep_down(down_kept)
    first_copy.wait()
    down_into(place_ref, (others_ref, mine_ref), first_kept, last_ref, down_kept)


def down_kernel(down_counts, place_ref, first_ref, last_ref, *refs):
    total = sum(down_counts)
    others_ref, mine_ref, first_kept, last_kept, staged, down_kept, sems, row_sems = refs[total:]
    downs = Staged(place_ref, grouped(refs[:total], down_counts), staged, sems)
    copies = [
        pltpu.make_async_copy(first_ref, first_kept, row_sems.at[0]),
        pltpu.make_async_copy(last_ref, last_kept, row_sems.at[1]),
    ]
    for copy in copies:
        copy.start()
    downs.keep_down(down_kept)
    for copy in copies:
        copy.wait()
    down_into(place_ref, (others_ref, mine_ref), first_kept, last_kept, down_kept)


def whole(*shape):
    return pl.BlockSpec(shape, lambda: (0,) * len(shape))


def kernel_call(kernel, place, arrays, outs, scratch):
    return pl.pallas_call(
        kernel,
        out_shape=[jax.ShapeDtypeStruct(shape, jnp.bfloat16) for shape in outs],
        in_specs=[pl.BlockSpec(memory_space=pltpu.SMEM)]
        + [pl.BlockSpec(memory_space=pltpu.HBM)] * len(arrays),
        out_specs=[whole(*shape) for shape in outs],
        scratch_shapes=scratch,
        compiler_params=pltpu.CompilerParams(vmem_limit_bytes=ALL_VMEM_BYTES),
        cost_estimate=pl.CostEstimate(flops=1000000, bytes_accessed=100000, transcendentals=0),
    )(place, *arrays)


def vmem(*shape):
    return pltpu.VMEM(shape, jnp.bfloat16)


def flat(sources):
    return [array for source in sources for array in source]


def early_hidden(place, rows, sources, own):
    units = (1 + len(sources) // 4) * UNITS
    scratch = [
        vmem(2 * ROWS, 2 * SPLIT),
        vmem(2, UNITS, 2 * SPLIT),
        vmem(len(sources), UNITS, SPLIT),
        vmem(units, 2 * SPLIT),
        vmem(units, 2 * SPLIT),
        pltpu.SemaphoreType.DMA((len(sources),)),
        pltpu.SemaphoreType.DMA((4,)),
    ]
    kernel = functools.partial(early_kernel, [len(source) for source in sources])
    return kernel_call(kernel, place, [rows, *flat(sources), *own], [(2 * ROWS, units)], scratch)[0]


def late_products(place, rows, first, sources, down_sources):
    scratch = [
        vmem(2 * ROWS, 2 * SPLIT),
        vmem(*first.shape),
        vmem(8, UNITS, SPLIT),
        vmem(UNITS, 2 * SPLIT),
        vmem(UNITS, 2 * SPLIT),
        vmem(4 * UNITS, SPLIT),
        pltpu.SemaphoreType.DMA((8,)),
        pltpu.SemaphoreType.DMA((3,)),
    ]
    kernel = functools.partial(late_kernel, [len(source) for source in sources], [len(source) for source in down_sources])
    arrays = [rows, first, *flat(sources), *flat(down_sources)]
    return kernel_call(kernel, place, arrays, [(ROWS, SPLIT), (ROWS, SPLIT), (2 * ROWS, UNITS)], scratch)


def down_products(place, first, last, down_sources):
    scratch = [
        vmem(*first.shape),
        vmem(*last.shape),
        vmem(4, UNITS, SPLIT),
        vmem(4 * UNITS, SPLIT),
        pltpu.SemaphoreType.DMA((4,)),
        pltpu.SemaphoreType.DMA((2,)),
    ]
    kernel = functools.partial(down_kernel, [len(source) for source in down_sources])
    return kernel_call(kernel, place, [first, last, *flat(down_sources)], [(ROWS, SPLIT)] * 2, scratch)


def spread_kernel(place_ref, places_ref, share_ref, *refs):
    out_ref = refs[-1]
    here = pl.multiple_of(place_ref[2] * SPLIT, SPLIT)
    places = places_ref[...]
    for index, lanes in enumerate((pl.ds(here, SPLIT), pl.ds(SPLIT - here, SPLIT))):
        if index == 0:
            parts = [refs[0][...]]
        else:
            expert_out = refs[1][...] + refs[2][...].astype(jnp.float32) + refs[3][...].astype(jnp.float32)
            high = expert_out.astype(jnp.bfloat16)
            parts = [high, (expert_out - high.astype(jnp.float32)).astype(jnp.bfloat16)]
        picked = [jnp.dot(places, part, preferred_element_type=jnp.float32) for part in parts]
        out_ref[:, lanes] = (share_ref[...] * sum(picked[1:], picked[0])).astype(jnp.bfloat16)


def spread(place, places, share, terms):
    block = lambda shape: pl.BlockSpec(shape, lambda i, place: (i, 0))
    return pl.pallas_call(
        spread_kernel,
        out_shape=jax.ShapeDtypeStruct((SPANS * CT, 2 * SPLIT), jnp.bfloat16),
        grid_spec=pltpu.PrefetchScalarGridSpec(
            num_scalar_prefetch=1,
            grid=(SPANS,),
            in_specs=[block((CT, CAP)), block((CT, 1))] + [block((CAP, term.shape[1])) for term in terms],
            out_specs=block((CT, 2 * SPLIT)),
        ),
        compiler_params=pltpu.CompilerParams(vmem_limit_bytes=ALL_VMEM_BYTES),
    )(place, places, share, *terms)


def on_device(tokens, expert_ids, gate_probs, gate_weight, up_weight, down_weight):
    model_width = tokens.shape[1]
    z_lo, y, core, x = (lax.axis_index(name) for name in ("z_lo", "y", "core", "x"))
    first = z_lo != core
    half = y % 2

    is_window = expert_ids == 0
    routed = jnp.any(is_window, axis=1)
    gate_share = jnp.sum(jnp.where(is_window, gate_probs, 0.0), axis=1)
    routed_blocks = routed.reshape(SPANS, CT)
    slot_place = jnp.cumsum(routed_blocks.astype(jnp.int32), axis=1) - 1
    selector = (
        slot_place[:, None, :] == jnp.arange(CAP, dtype=jnp.int32)[None, :, None]
    ) & routed_blocks[:, None, :]
    slot_rows = jnp.einsum(
        "bst,btd->bsd",
        selector.astype(jnp.bfloat16),
        tokens.reshape(SPANS, CT, model_width),
        preferred_element_type=jnp.float32,
    ).astype(jnp.bfloat16).reshape(SPANS * CAP, model_width)
    near_units, far_units = core * UNITS, (1 - core) * UNITS

    def piece(array, start, side):
        return lax.dynamic_slice(array, (start, side * SPLIT), (UNITS, SPLIT))

    shard = [gate_weight.T, up_weight.T, down_weight]
    order = [(0, near_units), (1, near_units), (2, near_units), (0, far_units), (1, far_units), (2, far_units)]
    own = [piece(shard[0], near_units, half)]
    place = jnp.stack([first.astype(jnp.int32), core, half])

    def joined(*parts):
        return jnp.concatenate(parts, axis=0)

    def pick(parts, index):
        return (parts[index], parts[index + 2])

    from_z, from_y = [], []
    work = slot_rows
    for step in range(13):
        if step < 5:
            feed = own[step]
        elif step < 7:
            feed = from_z[step - 3]
        elif step < 9:
            feed = own[5] if step == 7 else from_z[4]
        if step < 2:
            block = feed
        elif step < 9:
            block = jnp.where(first, feed, from_z[step - 2])
        else:
            block = from_z[step - 2]
        landed = max(step - 1, 0)
        settled = from_y[max(step - 4, 0) : max(step - 3, 0)]
        if step == 8:
            work["rows"] = rows
        block, from_z[:landed], settled, own, shard, work = lax.optimization_barrier(
            (block, from_z[:landed], settled, own, shard, work)
        )
        if step >= 4:
            from_y[step - 4] = settled[0]
        if step == 0:
            own.append(piece(shard[order[1][0]], order[1][1], half))
        if step == 1:
            own += [piece(shard[which], start, half) for which, start in order[2:]]
            work["own"] = [lax.dynamic_slice_in_dim(array, near_units, UNITS, 0) for array in shard[:2]]
            work["down"] = [piece(shard[2], near_units, side) for side in (half, 1 - half)]
            work["place"] = place
        if step < 11:
            from_z.append(moved(block, along_z))
        if step >= 2:
            from_y.append(moved(from_z[step - 2], along_y))
        if step == 0:
            rows = lax.all_gather(work, ("core", "x"), axis=0, tiled=True)
            work = {}
        def block_at(index):
            return [pick(from_z, index), pick(from_y, index), pick(from_z, index + 1), pick(from_y, index + 1)]

        if step == 10:
            work["hidden"] = early_hidden(work["place"], work["rows"], block_at(0) + block_at(3), work["own"])

    def downs(side, parts):
        return [(work["down"][side],), pick(parts, 2), pick(parts, 7), pick(parts, 8)]

    others_here, mine_here, last = late_products(work["place"], work["rows"], work["hidden"], block_at(5), downs(0, from_z))
    others_here, last, from_y[9], from_y[10] = lax.optimization_barrier((others_here, last, from_y[9], from_y[10]))
    sums_here = (mine_here.astype(jnp.float32) + moved(others_here, other_core).astype(jnp.float32)).astype(jnp.bfloat16)
    out_here = lax.psum_scatter(sums_here, "x", scatter_dimension=0, tiled=True)
    others_there, mine_there = down_products(work["place"], work["hidden"], last, downs(1, from_y))
    pair_there = (mine_there, moved(others_there, other_core))

    def summed(pair, step):
        start = (x + step) % 4 * (SPANS * CAP)
        first_part, second_part = (lax.dynamic_slice_in_dim(part, start, SPANS * CAP, 0) for part in pair)
        return first_part.astype(jnp.float32) + second_part.astype(jnp.float32)

    half_rows = SPANS * CAP // 2

    def far_pieces(pair):
        piece_on = summed(pair, 2).astype(jnp.bfloat16)
        return piece_on[:half_rows], piece_on[half_rows:]

    def far(pieces):
        return moved(pieces[0], along_x(1)), moved(pieces[1], along_x(3))

    def near(pair, arrived):
        above, below = summed(pair, 1), summed(pair, 3)
        above = joined(above[:half_rows] + arrived[0].astype(jnp.float32), above[half_rows:]).astype(jnp.bfloat16)
        below = joined(below[:half_rows], below[half_rows:] + arrived[1].astype(jnp.float32)).astype(jnp.bfloat16)
        return [moved(above, along_x(1)), moved(below, along_x(3))]

    pieces_there, pair_there = lax.optimization_barrier((far_pieces(pair_there), pair_there))
    near_there = near(pair_there, far(pieces_there))
    terms = [out_here, summed(pair_there, 0), *near_there]
    places = jnp.swapaxes(selector, 1, 2).reshape(SPANS * CT, CAP).astype(jnp.bfloat16)
    return spread(work["place"], places, gate_share[:, None], terms)


def solution(mesh):
    grid = Mesh(mesh.devices.reshape(SIZES), AXES)
    shard = ("z_hi", "x")
    in_specs = (
        P(AXES, None),
        P(AXES, None),
        P(AXES, None),
        P(None, shard),
        P(None, shard),
        P(shard, None),
    )
    return jax.shard_map(
        on_device, mesh=grid, in_specs=in_specs, out_specs=P(AXES, None), check_vma=False
    )
```

```python
import functools

import jax
import jax.numpy as jnp
import numpy as np
from jax import lax
from jax.experimental import pallas as pl
from jax.experimental.pallas import tpu as pltpu
from jax.sharding import Mesh, PartitionSpec as P

SPANS = 4
CT = 128
CAP = 32
AXES = ("z_lo", "y", "core", "z_hi", "x")
SIZES = (2, 4, 2, 4, 4)
UNITS = 168
SPLIT = 1536
ROWS = 512
ALL_VMEM_BYTES = 60 * 1024 * 1024


def moved(value, target):
    pairs = []
    for source in range(int(np.prod(SIZES))):
        z_lo, y, core, z_hi, x = (int(i) for i in np.unravel_index(source, SIZES))
        z = 2 * z_hi + z_lo
        z, y, core, x = target(z, y, core, x)
        z, y, core, x = z % 8, y % 4, core % 2, x % 4
        pairs.append((source, int(np.ravel_multi_index((z % 2, y, core, z // 2, x), SIZES))))
    return lax.ppermute(value, AXES, pairs)


def along_z(z, y, core, x):
    return z + 1 - 2 * core, y, core, x


def along_y(z, y, core, x):
    return z, y + 1 - 2 * core, core, x


def other_core(z, y, core, x):
    return z, y, 1 - core, x


def along_x(step):
    return lambda z, y, core, x: (z, y, core, x + step)


def grouped(refs, counts):
    refs = list(refs)
    return [[refs.pop(0) for _ in range(count)] for count in counts]


class Staged:
    def __init__(self, place_ref, sources, staged, sems):
        self.sources, self.staged, self.sems = sources, staged, sems
        feeds = place_ref[0] == 1
        for option in (0, 1):

            @pl.when(feeds == (option == 1))
            def _(option=option):
                for index in range(len(sources)):
                    self.copy(index, option).start()

    def copy(self, index, option):
        options = self.sources[index]
        option = min(option, len(options) - 1)
        return pltpu.make_async_copy(options[option], self.staged.at[index], self.sems.at[index])

    def keep_units(self, place_ref, kept, owned=0):
        here = pl.multiple_of(place_ref[2] * SPLIT, SPLIT)
        lanes = [pl.ds(here, SPLIT), pl.ds(SPLIT - here, SPLIT)]
        for index in range(len(self.sources)):
            self.copy(index, 0).wait()
            start = (owned + index // 4) * UNITS
            kept[index // 2 % 2][start : start + UNITS, lanes[index % 2]] = self.staged[index]

    def keep_down(self, kept):
        for index in range(len(self.sources)):
            self.copy(index, 0).wait()
            kept[index * UNITS : (index + 1) * UNITS, :] = self.staged[index]


SPANS_OF_ROWS = [pl.ds(start, ROWS) for start in range(0, 2 * ROWS, ROWS)]


def row_copies(rows_ref, rows_kept, sems):
    return [
        pltpu.make_async_copy(rows_ref.at[span], rows_kept.at[span], sems.at[index])
        for index, span in enumerate(SPANS_OF_ROWS)
    ]


def hidden_rows(copies, rows_kept, gate_kept, up_kept, out_ref):
    copies[0].wait()

    @pl.loop(0, 2 * ROWS, step=ROWS)
    def _(start):
        @pl.when(start == ROWS)
        def _():
            copies[1].wait()

        span = pl.ds(pl.multiple_of(start, ROWS), ROWS)
        gate_pre, up_pre = (
            lax.dot_general(
                rows_kept[span, :], kept[...], (((1,), (1,)), ((), ())), preferred_element_type=jnp.float32
            )
            for kept in (gate_kept, up_kept)
        )
        out_ref[span, :] = (gate_pre / (1.0 + jnp.exp(-gate_pre)) * up_pre).astype(jnp.bfloat16)


def early_kernel(counts, place_ref, rows_ref, *refs):
    total = sum(counts)
    own_refs, (out_ref, rows_kept, own_kept, staged, gate_kept, up_kept, sems, row_sems) = refs[total : total + 2], refs[total + 2 :]
    own_copies = [
        pltpu.make_async_copy(own_refs[index], own_kept.at[index], row_sems.at[2 + index]) for index in (0, 1)
    ]
    for copy in own_copies:
        copy.start()
    blocks = Staged(place_ref, grouped(refs[:total], counts), staged, sems)
    copies = row_copies(rows_ref, rows_kept, row_sems)
    for copy in copies:
        copy.start()
    for index, kept in enumerate((gate_kept, up_kept)):
        own_copies[index].wait()
        kept[:UNITS, :] = own_kept[index]
    blocks.keep_units(place_ref, (gate_kept, up_kept), owned=1)
    hidden_rows(copies, rows_kept, gate_kept, up_kept, out_ref)


def down_into(place_ref, outs, first, last, kept):
    core = place_ref[1]
    for owner, out_ref in zip((1 - core, core), outs):
        span = pl.ds(pl.multiple_of(owner * ROWS, ROWS), ROWS)
        units = jnp.concatenate([first[span, :], last[span, :]], axis=1)
        out_ref[...] = jnp.dot(units, kept[...], preferred_element_type=jnp.float32).astype(jnp.bfloat16)


def late_kernel(unit_counts, down_counts, place_ref, rows_ref, first_ref, *refs):
    split = sum(unit_counts)
    total = split + sum(down_counts)
    others_ref, mine_ref, last_ref = refs[total : total + 3]
    rows_kept, first_kept, staged, gate_kept, up_kept, down_kept, sems, row_sems = refs[total + 3 :]
    units = len(unit_counts)
    blocks = Staged(place_ref, grouped(refs[:split], unit_counts), staged.at[pl.ds(0, units)], sems.at[pl.ds(0, units)])
    copies = row_copies(rows_ref, rows_kept, row_sems)
    for copy in copies:
        copy.start()
    downs = Staged(
        place_ref, grouped(refs[split:total], down_counts), staged.at[pl.ds(units, 4)], sems.at[pl.ds(units, 4)]
    )
    first_copy = pltpu.make_async_copy(first_ref, first_kept, row_sems.at[2])
    first_copy.start()
    blocks.keep_units(place_ref, (gate_kept, up_kept))
    hidden_rows(copies, rows_kept, gate_kept, up_kept, last_ref)
    downs.keep_down(down_kept)
    first_copy.wait()
    down_into(place_ref, (others_ref, mine_ref), first_kept, last_ref, down_kept)


def down_kernel(down_counts, place_ref, first_ref, last_ref, *refs):
    total = sum(down_counts)
    others_ref, mine_ref, first_kept, last_kept, staged, down_kept, sems, row_sems = refs[total:]
    downs = Staged(place_ref, grouped(refs[:total], down_counts), staged, sems)
    copies = [
        pltpu.make_async_copy(first_ref, first_kept, row_sems.at[0]),
        pltpu.make_async_copy(last_ref, last_kept, row_sems.at[1]),
    ]
    for copy in copies:
        copy.start()
    downs.keep_down(down_kept)
    for copy in copies:
        copy.wait()
    down_into(place_ref, (others_ref, mine_ref), first_kept, last_kept, down_kept)


def whole(*shape):
    return pl.BlockSpec(shape, lambda: (0,) * len(shape))


def kernel_call(kernel, place, arrays, outs, scratch):
    return pl.pallas_call(
        kernel,
        out_shape=[jax.ShapeDtypeStruct(shape, jnp.bfloat16) for shape in outs],
        in_specs=[pl.BlockSpec(memory_space=pltpu.SMEM)]
        + [pl.BlockSpec(memory_space=pltpu.HBM)] * len(arrays),
        out_specs=[whole(*shape) for shape in outs],
        scratch_shapes=scratch,
        compiler_params=pltpu.CompilerParams(vmem_limit_bytes=ALL_VMEM_BYTES),
        cost_estimate=pl.CostEstimate(flops=1000000, bytes_accessed=100000, transcendentals=0),
    )(place, *arrays)


def vmem(*shape):
    return pltpu.VMEM(shape, jnp.bfloat16)


def flat(sources):
    return [array for source in sources for array in source]


def early_hidden(place, rows, sources, own):
    units = (1 + len(sources) // 4) * UNITS
    scratch = [
        vmem(2 * ROWS, 2 * SPLIT),
        vmem(2, UNITS, 2 * SPLIT),
        vmem(len(sources), UNITS, SPLIT),
        vmem(units, 2 * SPLIT),
        vmem(units, 2 * SPLIT),
        pltpu.SemaphoreType.DMA((len(sources),)),
        pltpu.SemaphoreType.DMA((4,)),
    ]
    kernel = functools.partial(early_kernel, [len(source) for source in sources])
    return kernel_call(kernel, place, [rows, *flat(sources), *own], [(2 * ROWS, units)], scratch)[0]


def late_products(place, rows, first, sources, down_sources):
    scratch = [
        vmem(2 * ROWS, 2 * SPLIT),
        vmem(*first.shape),
        vmem(8, UNITS, SPLIT),
        vmem(UNITS, 2 * SPLIT),
        vmem(UNITS, 2 * SPLIT),
        vmem(4 * UNITS, SPLIT),
        pltpu.SemaphoreType.DMA((8,)),
        pltpu.SemaphoreType.DMA((3,)),
    ]
    kernel = functools.partial(late_kernel, [len(source) for source in sources], [len(source) for source in down_sources])
    arrays = [rows, first, *flat(sources), *flat(down_sources)]
    return kernel_call(kernel, place, arrays, [(ROWS, SPLIT), (ROWS, SPLIT), (2 * ROWS, UNITS)], scratch)


def down_products(place, first, last, down_sources):
    scratch = [
        vmem(*first.shape),
        vmem(*last.shape),
        vmem(4, UNITS, SPLIT),
        vmem(4 * UNITS, SPLIT),
        pltpu.SemaphoreType.DMA((4,)),
        pltpu.SemaphoreType.DMA((2,)),
    ]
    kernel = functools.partial(down_kernel, [len(source) for source in down_sources])
    return kernel_call(kernel, place, [first, last, *flat(down_sources)], [(ROWS, SPLIT)] * 2, scratch)


def spread_kernel(place_ref, places_ref, share_ref, *refs):
    out_ref = refs[-1]
    here = pl.multiple_of(place_ref[2] * SPLIT, SPLIT)
    places = places_ref[...]
    for index, lanes in enumerate((pl.ds(here, SPLIT), pl.ds(SPLIT - here, SPLIT))):
        if index == 0:
            parts = [refs[0][...]]
        else:
            expert_out = sum((ref[...].astype(jnp.float32) for ref in refs[2:5]), refs[1][...].astype(jnp.float32))
            high = expert_out.astype(jnp.bfloat16)
            parts = [high, (expert_out - high.astype(jnp.float32)).astype(jnp.bfloat16)]
        picked = [jnp.dot(places, part, preferred_element_type=jnp.float32) for part in parts]
        out_ref[:, lanes] = (share_ref[...] * sum(picked[1:], picked[0])).astype(jnp.bfloat16)


def spread(place, places, share, pair, terms):
    def block(*shape):
        return pl.BlockSpec(shape, lambda i, place: (i, 0))

    own = pl.BlockSpec((CAP, SPLIT), lambda i, place: (place[3] * SPANS + i, 0))
    return pl.pallas_call(
        spread_kernel,
        out_shape=jax.ShapeDtypeStruct((SPANS * CT, 2 * SPLIT), jnp.bfloat16),
        grid_spec=pltpu.PrefetchScalarGridSpec(
            num_scalar_prefetch=1,
            grid=(SPANS,),
            in_specs=[block(CT, CAP), block(CT, 1), block(CAP, SPLIT), own, own, block(CAP, SPLIT), block(CAP, SPLIT)],
            out_specs=block(CT, 2 * SPLIT),
        ),
        compiler_params=pltpu.CompilerParams(vmem_limit_bytes=ALL_VMEM_BYTES),
    )(place, places, share, terms[0], *pair, *terms[1:])


def on_device(tokens, expert_ids, gate_probs, gate_weight, up_weight, down_weight):
    model_width = tokens.shape[1]
    z_lo, y, core, x = (lax.axis_index(name) for name in ("z_lo", "y", "core", "x"))
    first = z_lo != core
    half = y % 2

    is_window = expert_ids == 0
    routed = jnp.any(is_window, axis=1)
    gate_share = jnp.sum(jnp.where(is_window, gate_probs, 0.0), axis=1)
    routed_blocks = routed.reshape(SPANS, CT)
    slot_place = jnp.cumsum(routed_blocks.astype(jnp.int32), axis=1) - 1
    selector = (
        slot_place[:, None, :] == jnp.arange(CAP, dtype=jnp.int32)[None, :, None]
    ) & routed_blocks[:, None, :]
    slot_rows = jnp.einsum(
        "bst,btd->bsd",
        selector.astype(jnp.bfloat16),
        tokens.reshape(SPANS, CT, model_width),
        preferred_element_type=jnp.float32,
    ).astype(jnp.bfloat16).reshape(SPANS * CAP, model_width)
    near_units, far_units = core * UNITS, (1 - core) * UNITS

    def piece(array, start, side):
        return lax.dynamic_slice(array, (start, side * SPLIT), (UNITS, SPLIT))

    shard = [gate_weight.T, up_weight.T, down_weight]
    order = [(0, near_units), (1, near_units), (2, near_units), (0, far_units), (1, far_units), (2, far_units)]
    own = [piece(shard[0], near_units, half)]
    place = jnp.stack([first.astype(jnp.int32), core, half, x])

    def joined(*parts):
        return jnp.concatenate(parts, axis=0)

    def pick(parts, index):
        return (parts[index], parts[index + 2])

    from_z, from_y = [], []
    work = slot_rows
    for step in range(13):
        if step < 5:
            feed = own[step]
        elif step < 7:
            feed = from_z[step - 3]
        elif step < 9:
            feed = own[5] if step == 7 else from_z[4]
        if step < 2:
            block = feed
        elif step < 9:
            block = jnp.where(first, feed, from_z[step - 2])
        else:
            block = from_z[step - 2]
        landed = max(step - 1, 0)
        settled = from_y[max(step - 4, 0) : max(step - 3, 0)]
        if step == 8:
            work["rows"] = rows
        block, from_z[:landed], settled, own, shard, work = lax.optimization_barrier(
            (block, from_z[:landed], settled, own, shard, work)
        )
        if step >= 4:
            from_y[step - 4] = settled[0]
        if step == 0:
            own.append(piece(shard[order[1][0]], order[1][1], half))
        if step == 1:
            own += [piece(shard[which], start, half) for which, start in order[2:]]
            work["own"] = [lax.dynamic_slice_in_dim(array, near_units, UNITS, 0) for array in shard[:2]]
            work["down"] = [piece(shard[2], near_units, side) for side in (half, 1 - half)]
            work["place"] = place
        if step < 11:
            from_z.append(moved(block, along_z))
        if step >= 2:
            from_y.append(moved(from_z[step - 2], along_y))
        if step == 0:
            rows = lax.all_gather(work, ("core", "x"), axis=0, tiled=True)
            work = {}
        def block_at(index):
            return [pick(from_z, index), pick(from_y, index), pick(from_z, index + 1), pick(from_y, index + 1)]

        if step == 10:
            work["hidden"] = early_hidden(work["place"], work["rows"], block_at(0) + block_at(3), work["own"])

    def downs(side, parts):
        return [(work["down"][side],), pick(parts, 2), pick(parts, 7), pick(parts, 8)]

    others_here, mine_here, last = late_products(work["place"], work["rows"], work["hidden"], block_at(5), downs(0, from_z))
    others_here, last, from_y[9], from_y[10] = lax.optimization_barrier((others_here, last, from_y[9], from_y[10]))
    sums_here = (mine_here.astype(jnp.float32) + moved(others_here, other_core).astype(jnp.float32)).astype(jnp.bfloat16)
    out_here = lax.psum_scatter(sums_here, "x", scatter_dimension=0, tiled=True)
    others_there, mine_there = down_products(work["place"], work["hidden"], last, downs(1, from_y))
    pair_there = (mine_there, moved(others_there, other_core))

    def summed(pair, step):
        start = (x + step) % 4 * (SPANS * CAP)
        first_part, second_part = (lax.dynamic_slice_in_dim(part, start, SPANS * CAP, 0) for part in pair)
        return first_part.astype(jnp.float32) + second_part.astype(jnp.float32)

    half_rows = SPANS * CAP // 2

    def far_pieces(pair):
        piece_on = summed(pair, 2).astype(jnp.bfloat16)
        return piece_on[:half_rows], piece_on[half_rows:]

    def far(pieces):
        return moved(pieces[0], along_x(1)), moved(pieces[1], along_x(3))

    def near(pair, arrived):
        above, below = summed(pair, 1), summed(pair, 3)
        above = joined(above[:half_rows] + arrived[0].astype(jnp.float32), above[half_rows:]).astype(jnp.bfloat16)
        below = joined(below[:half_rows], below[half_rows:] + arrived[1].astype(jnp.float32)).astype(jnp.bfloat16)
        return [moved(above, along_x(1)), moved(below, along_x(3))]

    pieces_there, pair_there = lax.optimization_barrier((far_pieces(pair_there), pair_there))
    near_there = near(pair_there, far(pieces_there))
    terms = [out_here, *near_there]
    places = jnp.swapaxes(selector, 1, 2).reshape(SPANS * CT, CAP).astype(jnp.bfloat16)
    return spread(work["place"], places, gate_share[:, None], pair_there, terms)


def solution(mesh):
    grid = Mesh(mesh.devices.reshape(SIZES), AXES)
    shard = ("z_hi", "x")
    in_specs = (
        P(AXES, None),
        P(AXES, None),
        P(AXES, None),
        P(None, shard),
        P(None, shard),
        P(shard, None),
    )
    return jax.shard_map(
        on_device, mesh=grid, in_specs=in_specs, out_specs=P(AXES, None), check_vma=False
    )
```

```python
import functools

import jax
import jax.numpy as jnp
import numpy as np
from jax import lax
from jax.experimental import pallas as pl
from jax.experimental.pallas import tpu as pltpu
from jax.sharding import Mesh, PartitionSpec as P

SPANS = 4
CT = 128
CAP = 32
AXES = ("z_lo", "y", "core", "z_hi", "x")
SIZES = (2, 4, 2, 4, 4)
UNITS = 168
SPLIT = 1536
ROWS = 512
ALL_VMEM_BYTES = 60 * 1024 * 1024


def moved(value, target):
    pairs = []
    for source in range(int(np.prod(SIZES))):
        z_lo, y, core, z_hi, x = (int(i) for i in np.unravel_index(source, SIZES))
        z = 2 * z_hi + z_lo
        z, y, core, x = target(z, y, core, x)
        z, y, core, x = z % 8, y % 4, core % 2, x % 4
        pairs.append((source, int(np.ravel_multi_index((z % 2, y, core, z // 2, x), SIZES))))
    return lax.ppermute(value, AXES, pairs)


def along_z(z, y, core, x):
    return z + 1 - 2 * core, y, core, x


def along_y(z, y, core, x):
    return z, y + 1 - 2 * core, core, x


def other_core(z, y, core, x):
    return z, y, 1 - core, x


def along_x(step):
    return lambda z, y, core, x: (z, y, core, x + step)


def grouped(refs, counts):
    refs = list(refs)
    return [[refs.pop(0) for _ in range(count)] for count in counts]


class Staged:
    def __init__(self, place_ref, sources, staged, sems):
        self.sources, self.staged, self.sems = sources, staged, sems
        feeds = place_ref[0] == 1
        for option in (0, 1):

            @pl.when(feeds == (option == 1))
            def _(option=option):
                for index in range(len(sources)):
                    self.copy(index, option).start()

    def copy(self, index, option):
        options = self.sources[index]
        option = min(option, len(options) - 1)
        return pltpu.make_async_copy(options[option], self.staged.at[index], self.sems.at[index])

    def keep_units(self, place_ref, kept, owned=0):
        here = pl.multiple_of(place_ref[2] * SPLIT, SPLIT)
        lanes = [pl.ds(here, SPLIT), pl.ds(SPLIT - here, SPLIT)]
        for index in range(len(self.sources)):
            self.copy(index, 0).wait()
            start = (owned + index // 4) * UNITS
            kept[index // 2 % 2][start : start + UNITS, lanes[index % 2]] = self.staged[index]

    def keep_down(self, kept):
        for index in range(len(self.sources)):
            self.copy(index, 0).wait()
            kept[index * UNITS : (index + 1) * UNITS, :] = self.staged[index]


SPANS_OF_ROWS = [pl.ds(start, ROWS) for start in range(0, 2 * ROWS, ROWS)]


def row_copies(rows_ref, rows_kept, sems):
    return [
        pltpu.make_async_copy(rows_ref.at[span], rows_kept.at[span], sems.at[index])
        for index, span in enumerate(SPANS_OF_ROWS)
    ]


def hidden_rows(copies, rows_kept, gate_kept, up_kept, out_ref):
    copies[0].wait()

    @pl.loop(0, 2 * ROWS, step=ROWS)
    def _(start):
        @pl.when(start == ROWS)
        def _():
            copies[1].wait()

        span = pl.ds(pl.multiple_of(start, ROWS), ROWS)
        gate_pre, up_pre = (
            lax.dot_general(
                rows_kept[span, :], kept[...], (((1,), (1,)), ((), ())), preferred_element_type=jnp.float32
            )
            for kept in (gate_kept, up_kept)
        )
        out_ref[span, :] = (gate_pre / (1.0 + jnp.exp(-gate_pre)) * up_pre).astype(jnp.bfloat16)


def early_kernel(counts, place_ref, rows_ref, *refs):
    total = sum(counts)
    own_refs, (out_ref, rows_kept, own_kept, staged, gate_kept, up_kept, sems, row_sems) = refs[total : total + 2], refs[total + 2 :]
    own_copies = [
        pltpu.make_async_copy(own_refs[index], own_kept.at[index], row_sems.at[2 + index]) for index in (0, 1)
    ]
    for copy in own_copies:
        copy.start()
    blocks = Staged(place_ref, grouped(refs[:total], counts), staged, sems)
    copies = row_copies(rows_ref, rows_kept, row_sems)
    for copy in copies:
        copy.start()
    for index, kept in enumerate((gate_kept, up_kept)):
        own_copies[index].wait()
        kept[:UNITS, :] = own_kept[index]
    blocks.keep_units(place_ref, (gate_kept, up_kept), owned=1)
    hidden_rows(copies, rows_kept, gate_kept, up_kept, out_ref)


def down_into(place_ref, outs, first, last, kept):
    core = place_ref[1]
    for owner, out_ref in zip((1 - core, core), outs):
        span = pl.ds(pl.multiple_of(owner * ROWS, ROWS), ROWS)
        units = jnp.concatenate([first[span, :], last[span, :]], axis=1)
        out_ref[...] = jnp.dot(units, kept[...], preferred_element_type=jnp.float32).astype(jnp.bfloat16)


def late_kernel(unit_counts, down_counts, place_ref, rows_ref, first_ref, *refs):
    split = sum(unit_counts)
    total = split + sum(down_counts)
    others_ref, mine_ref, last_ref = refs[total : total + 3]
    rows_kept, first_kept, staged, gate_kept, up_kept, down_kept, sems, row_sems = refs[total + 3 :]
    units = len(unit_counts)
    blocks = Staged(place_ref, grouped(refs[:split], unit_counts), staged.at[pl.ds(0, units)], sems.at[pl.ds(0, units)])
    copies = row_copies(rows_ref, rows_kept, row_sems)
    for copy in copies:
        copy.start()
    downs = Staged(
        place_ref, grouped(refs[split:total], down_counts), staged.at[pl.ds(units, 4)], sems.at[pl.ds(units, 4)]
    )
    first_copy = pltpu.make_async_copy(first_ref, first_kept, row_sems.at[2])
    first_copy.start()
    blocks.keep_units(place_ref, (gate_kept, up_kept))
    hidden_rows(copies, rows_kept, gate_kept, up_kept, last_ref)
    downs.keep_down(down_kept)
    first_copy.wait()
    down_into(place_ref, (others_ref, mine_ref), first_kept, last_ref, down_kept)


def down_kernel(down_counts, place_ref, first_ref, last_ref, *refs):
    total = sum(down_counts)
    others_ref, mine_ref, first_kept, last_kept, staged, down_kept, sems, row_sems = refs[total:]
    downs = Staged(place_ref, grouped(refs[:total], down_counts), staged, sems)
    copies = [
        pltpu.make_async_copy(first_ref, first_kept, row_sems.at[0]),
        pltpu.make_async_copy(last_ref, last_kept, row_sems.at[1]),
    ]
    for copy in copies:
        copy.start()
    downs.keep_down(down_kept)
    for copy in copies:
        copy.wait()
    down_into(place_ref, (others_ref, mine_ref), first_kept, last_kept, down_kept)


def whole(*shape):
    return pl.BlockSpec(shape, lambda: (0,) * len(shape))


def kernel_call(kernel, place, arrays, outs, scratch):
    return pl.pallas_call(
        kernel,
        out_shape=[jax.ShapeDtypeStruct(shape, jnp.bfloat16) for shape in outs],
        in_specs=[pl.BlockSpec(memory_space=pltpu.SMEM)]
        + [pl.BlockSpec(memory_space=pltpu.HBM)] * len(arrays),
        out_specs=[whole(*shape) for shape in outs],
        scratch_shapes=scratch,
        compiler_params=pltpu.CompilerParams(vmem_limit_bytes=ALL_VMEM_BYTES),
        cost_estimate=pl.CostEstimate(flops=1000000, bytes_accessed=100000, transcendentals=0),
    )(place, *arrays)


def vmem(*shape):
    return pltpu.VMEM(shape, jnp.bfloat16)


def flat(sources):
    return [array for source in sources for array in source]


def early_hidden(place, rows, sources, own):
    units = (1 + len(sources) // 4) * UNITS
    scratch = [
        vmem(2 * ROWS, 2 * SPLIT),
        vmem(2, UNITS, 2 * SPLIT),
        vmem(len(sources), UNITS, SPLIT),
        vmem(units, 2 * SPLIT),
        vmem(units, 2 * SPLIT),
        pltpu.SemaphoreType.DMA((len(sources),)),
        pltpu.SemaphoreType.DMA((4,)),
    ]
    kernel = functools.partial(early_kernel, [len(source) for source in sources])
    return kernel_call(kernel, place, [rows, *flat(sources), *own], [(2 * ROWS, units)], scratch)[0]


def late_products(place, rows, first, sources, down_sources):
    scratch = [
        vmem(2 * ROWS, 2 * SPLIT),
        vmem(*first.shape),
        vmem(8, UNITS, SPLIT),
        vmem(UNITS, 2 * SPLIT),
        vmem(UNITS, 2 * SPLIT),
        vmem(4 * UNITS, SPLIT),
        pltpu.SemaphoreType.DMA((8,)),
        pltpu.SemaphoreType.DMA((3,)),
    ]
    kernel = functools.partial(late_kernel, [len(source) for source in sources], [len(source) for source in down_sources])
    arrays = [rows, first, *flat(sources), *flat(down_sources)]
    return kernel_call(kernel, place, arrays, [(ROWS, SPLIT), (ROWS, SPLIT), (2 * ROWS, UNITS)], scratch)


def down_products(place, first, last, down_sources):
    scratch = [
        vmem(*first.shape),
        vmem(*last.shape),
        vmem(4, UNITS, SPLIT),
        vmem(4 * UNITS, SPLIT),
        pltpu.SemaphoreType.DMA((4,)),
        pltpu.SemaphoreType.DMA((2,)),
    ]
    kernel = functools.partial(down_kernel, [len(source) for source in down_sources])
    return kernel_call(kernel, place, [first, last, *flat(down_sources)], [(ROWS, SPLIT)] * 2, scratch)


def spread_kernel(place_ref, places_ref, share_ref, *refs):
    out_ref = refs[-1]
    here = pl.multiple_of(place_ref[2] * SPLIT, SPLIT)
    places = places_ref[...]
    for index, lanes in enumerate((pl.ds(here, SPLIT), pl.ds(SPLIT - here, SPLIT))):
        if index == 0:
            picked = jnp.dot(places, refs[0][...], preferred_element_type=jnp.float32)
        else:
            expert_out = sum((ref[...].astype(jnp.float32) for ref in refs[2:5]), refs[1][...].astype(jnp.float32))
            high = expert_out.astype(jnp.bfloat16)
            low = (expert_out - high.astype(jnp.float32)).astype(jnp.bfloat16)
            picked = jnp.dot(
                jnp.concatenate([places, places], axis=1),
                jnp.concatenate([high, low], axis=0),
                preferred_element_type=jnp.float32,
            )
        out_ref[:, lanes] = (share_ref[...] * picked).astype(jnp.bfloat16)


def spread(place, places, share, pair, terms):
    def block(*shape):
        return pl.BlockSpec(shape, lambda i, place: (i, 0))

    slots = 2 * CAP
    own = pl.BlockSpec((slots, SPLIT), lambda i, place: (place[3] * (SPANS // 2) + i, 0))
    rows = block(slots, SPLIT)
    return pl.pallas_call(
        spread_kernel,
        out_shape=jax.ShapeDtypeStruct((SPANS * CT, 2 * SPLIT), jnp.bfloat16),
        grid_spec=pltpu.PrefetchScalarGridSpec(
            num_scalar_prefetch=1,
            grid=(SPANS // 2,),
            in_specs=[block(2 * CT, slots), block(2 * CT, 1), rows, own, own, rows, rows],
            out_specs=block(2 * CT, 2 * SPLIT),
        ),
        compiler_params=pltpu.CompilerParams(vmem_limit_bytes=ALL_VMEM_BYTES),
    )(place, places, share, terms[0], *pair, *terms[1:])


def on_device(tokens, expert_ids, gate_probs, gate_weight, up_weight, down_weight):
    model_width = tokens.shape[1]
    z_lo, y, core, x = (lax.axis_index(name) for name in ("z_lo", "y", "core", "x"))
    first = z_lo != core
    half = y % 2

    is_window = expert_ids == 0
    routed = jnp.any(is_window, axis=1)
    gate_share = jnp.sum(jnp.where(is_window, gate_probs, 0.0), axis=1)
    routed_blocks = routed.reshape(SPANS, CT)
    slot_place = jnp.cumsum(routed_blocks.astype(jnp.int32), axis=1) - 1
    selector = (
        slot_place[:, None, :] == jnp.arange(CAP, dtype=jnp.int32)[None, :, None]
    ) & routed_blocks[:, None, :]
    slot_rows = jnp.einsum(
        "bst,btd->bsd",
        selector.astype(jnp.bfloat16),
        tokens.reshape(SPANS, CT, model_width),
        preferred_element_type=jnp.float32,
    ).astype(jnp.bfloat16).reshape(SPANS * CAP, model_width)
    near_units, far_units = core * UNITS, (1 - core) * UNITS

    def piece(array, start, side):
        return lax.dynamic_slice(array, (start, side * SPLIT), (UNITS, SPLIT))

    shard = [gate_weight.T, up_weight.T, down_weight]
    order = [(0, near_units), (1, near_units), (2, near_units), (0, far_units), (1, far_units), (2, far_units)]
    own = [piece(shard[0], near_units, half)]
    place = jnp.stack([first.astype(jnp.int32), core, half, x])

    def joined(*parts):
        return jnp.concatenate(parts, axis=0)

    def pick(parts, index):
        return (parts[index], parts[index + 2])

    from_z, from_y = [], []
    work = slot_rows
    for step in range(13):
        if step < 5:
            feed = own[step]
        elif step < 7:
            feed = from_z[step - 3]
        elif step < 9:
            feed = own[5] if step == 7 else from_z[4]
        if step < 2:
            block = feed
        elif step < 9:
            block = jnp.where(first, feed, from_z[step - 2])
        else:
            block = from_z[step - 2]
        landed = max(step - 1, 0)
        settled = from_y[max(step - 4, 0) : max(step - 3, 0)]
        if step == 8:
            work["rows"] = rows
        block, from_z[:landed], settled, own, shard, work = lax.optimization_barrier(
            (block, from_z[:landed], settled, own, shard, work)
        )
        if step >= 4:
            from_y[step - 4] = settled[0]
        if step == 0:
            own.append(piece(shard[order[1][0]], order[1][1], half))
        if step == 1:
            own += [piece(shard[which], start, half) for which, start in order[2:]]
            work["own"] = [lax.dynamic_slice_in_dim(array, near_units, UNITS, 0) for array in shard[:2]]
            work["down"] = [piece(shard[2], near_units, side) for side in (half, 1 - half)]
            work["place"] = place
        if step < 11:
            from_z.append(moved(block, along_z))
        if step >= 2:
            from_y.append(moved(from_z[step - 2], along_y))
        if step == 0:
            rows = lax.all_gather(work, ("core", "x"), axis=0, tiled=True)
            work = {}
        def block_at(index):
            return [pick(from_z, index), pick(from_y, index), pick(from_z, index + 1), pick(from_y, index + 1)]

        if step == 10:
            work["hidden"] = early_hidden(work["place"], work["rows"], block_at(0) + block_at(3), work["own"])

    def downs(side, parts):
        return [(work["down"][side],), pick(parts, 2), pick(parts, 7), pick(parts, 8)]

    others_here, mine_here, last = late_products(work["place"], work["rows"], work["hidden"], block_at(5), downs(0, from_z))
    others_here, last, from_y[9], from_y[10] = lax.optimization_barrier((others_here, last, from_y[9], from_y[10]))
    sums_here = (mine_here.astype(jnp.float32) + moved(others_here, other_core).astype(jnp.float32)).astype(jnp.bfloat16)
    out_here = lax.psum_scatter(sums_here, "x", scatter_dimension=0, tiled=True)
    others_there, mine_there = down_products(work["place"], work["hidden"], last, downs(1, from_y))
    pair_there = (mine_there, moved(others_there, other_core))

    def summed(pair, step):
        start = (x + step) % 4 * (SPANS * CAP)
        first_part, second_part = (lax.dynamic_slice_in_dim(part, start, SPANS * CAP, 0) for part in pair)
        return first_part.astype(jnp.float32) + second_part.astype(jnp.float32)

    half_rows = SPANS * CAP // 2

    def far_pieces(pair):
        piece_on = summed(pair, 2).astype(jnp.bfloat16)
        return piece_on[:half_rows], piece_on[half_rows:]

    def far(pieces):
        return moved(pieces[0], along_x(1)), moved(pieces[1], along_x(3))

    def near(pair, arrived):
        above, below = summed(pair, 1), summed(pair, 3)
        above = joined(above[:half_rows] + arrived[0].astype(jnp.float32), above[half_rows:]).astype(jnp.bfloat16)
        below = joined(below[:half_rows], below[half_rows:] + arrived[1].astype(jnp.float32)).astype(jnp.bfloat16)
        return [moved(above, along_x(1)), moved(below, along_x(3))]

    pieces_there, pair_there = lax.optimization_barrier((far_pieces(pair_there), pair_there))
    near_there = near(pair_there, far(pieces_there))
    terms = [out_here, *near_there]
    pairs = jnp.swapaxes(selector, 1, 2).reshape(SPANS // 2, 2, CT, 1, CAP)
    pairs = pairs & jnp.eye(2, dtype=bool)[None, :, None, :, None]
    places = pairs.reshape(SPANS * CT, 2 * CAP).astype(jnp.bfloat16)
    return spread(work["place"], places, gate_share[:, None], pair_there, terms)


def solution(mesh):
    grid = Mesh(mesh.devices.reshape(SIZES), AXES)
    shard = ("z_hi", "x")
    in_specs = (
        P(AXES, None),
        P(AXES, None),
        P(AXES, None),
        P(None, shard),
        P(None, shard),
        P(shard, None),
    )
    return jax.shard_map(
        on_device, mesh=grid, in_specs=in_specs, out_specs=P(AXES, None), check_vma=False
    )
```

```python
import functools

import jax
import jax.numpy as jnp
import numpy as np
from jax import lax
from jax.experimental import pallas as pl
from jax.experimental.pallas import tpu as pltpu
from jax.sharding import Mesh, PartitionSpec as P

SPANS = 4
CT = 128
CAP = 32
AXES = ("z_lo", "y", "core", "z_hi", "x")
SIZES = (2, 4, 2, 4, 4)
UNITS = 168
SPLIT = 1536
ROWS = 512
ALL_VMEM_BYTES = 60 * 1024 * 1024


def moved(value, target):
    pairs = []
    for source in range(int(np.prod(SIZES))):
        z_lo, y, core, z_hi, x = (int(i) for i in np.unravel_index(source, SIZES))
        z = 2 * z_hi + z_lo
        z, y, core, x = target(z, y, core, x)
        z, y, core, x = z % 8, y % 4, core % 2, x % 4
        pairs.append((source, int(np.ravel_multi_index((z % 2, y, core, z // 2, x), SIZES))))
    return lax.ppermute(value, AXES, pairs)


def along_z(z, y, core, x):
    return z + 1 - 2 * core, y, core, x


def along_y(z, y, core, x):
    return z, y + 1 - 2 * core, core, x


def other_core(z, y, core, x):
    return z, y, 1 - core, x


def along_x(step):
    return lambda z, y, core, x: (z, y, core, x + step)


def grouped(refs, counts):
    refs = list(refs)
    return [[refs.pop(0) for _ in range(count)] for count in counts]


class Staged:
    def __init__(self, place_ref, sources, staged, sems):
        self.sources, self.staged, self.sems = sources, staged, sems
        feeds = place_ref[0] == 1
        for option in (0, 1):

            @pl.when(feeds == (option == 1))
            def _(option=option):
                for index in range(len(sources)):
                    self.copy(index, option).start()

    def copy(self, index, option):
        options = self.sources[index]
        option = min(option, len(options) - 1)
        return pltpu.make_async_copy(options[option], self.staged.at[index], self.sems.at[index])

    def keep_units(self, place_ref, kept, owned=0):
        here = pl.multiple_of(place_ref[2] * SPLIT, SPLIT)
        lanes = [pl.ds(here, SPLIT), pl.ds(SPLIT - here, SPLIT)]
        for index in range(len(self.sources)):
            self.copy(index, 0).wait()
            start = (owned + index // 4) * UNITS
            kept[index // 2 % 2][start : start + UNITS, lanes[index % 2]] = self.staged[index]

    def keep_down(self, kept):
        for index in range(len(self.sources)):
            self.copy(index, 0).wait()
            kept[index * UNITS : (index + 1) * UNITS, :] = self.staged[index]


SPANS_OF_ROWS = [pl.ds(start, ROWS) for start in range(0, 2 * ROWS, ROWS)]


def row_copies(rows_ref, rows_kept, sems):
    return [
        pltpu.make_async_copy(rows_ref.at[span], rows_kept.at[span], sems.at[index])
        for index, span in enumerate(SPANS_OF_ROWS)
    ]


def hidden_rows(copies, rows_kept, gate_kept, up_kept, out_ref):
    copies[0].wait()

    @pl.loop(0, 2 * ROWS, step=ROWS)
    def _(start):
        @pl.when(start == ROWS)
        def _():
            copies[1].wait()

        span = pl.ds(pl.multiple_of(start, ROWS), ROWS)
        gate_pre, up_pre = (
            lax.dot_general(
                rows_kept[span, :], kept[...], (((1,), (1,)), ((), ())), preferred_element_type=jnp.float32
            )
            for kept in (gate_kept, up_kept)
        )
        out_ref[span, :] = (gate_pre / (1.0 + jnp.exp(-gate_pre)) * up_pre).astype(jnp.bfloat16)


def early_kernel(counts, place_ref, rows_ref, *refs):
    total = sum(counts)
    own_refs, (out_ref, rows_kept, own_kept, staged, gate_kept, up_kept, sems, row_sems) = refs[total : total + 2], refs[total + 2 :]
    own_copies = [
        pltpu.make_async_copy(own_refs[index], own_kept.at[index], row_sems.at[2 + index]) for index in (0, 1)
    ]
    for copy in own_copies:
        copy.start()
    blocks = Staged(place_ref, grouped(refs[:total], counts), staged, sems)
    copies = row_copies(rows_ref, rows_kept, row_sems)
    for copy in copies:
        copy.start()
    for index, kept in enumerate((gate_kept, up_kept)):
        own_copies[index].wait()
        kept[:UNITS, :] = own_kept[index]
    blocks.keep_units(place_ref, (gate_kept, up_kept), owned=1)
    hidden_rows(copies, rows_kept, gate_kept, up_kept, out_ref)


def down_into(place_ref, outs, first, last, kept):
    core = place_ref[1]
    for owner, out_ref in zip((1 - core, core), outs):
        span = pl.ds(pl.multiple_of(owner * ROWS, ROWS), ROWS)
        units = jnp.concatenate([first[span, :], last[span, :]], axis=1)
        out_ref[...] = jnp.dot(units, kept[...], preferred_element_type=jnp.float32).astype(jnp.bfloat16)


def late_kernel(unit_counts, down_counts, place_ref, rows_ref, first_ref, *refs):
    split = sum(unit_counts)
    total = split + sum(down_counts)
    others_ref, mine_ref, last_ref = refs[total : total + 3]
    rows_kept, first_kept, staged, gate_kept, up_kept, down_kept, sems, row_sems = refs[total + 3 :]
    units = len(unit_counts)
    blocks = Staged(place_ref, grouped(refs[:split], unit_counts), staged.at[pl.ds(0, units)], sems.at[pl.ds(0, units)])
    copies = row_copies(rows_ref, rows_kept, row_sems)
    for copy in copies:
        copy.start()
    downs = Staged(
        place_ref, grouped(refs[split:total], down_counts), staged.at[pl.ds(units, 4)], sems.at[pl.ds(units, 4)]
    )
    first_copy = pltpu.make_async_copy(first_ref, first_kept, row_sems.at[2])
    first_copy.start()
    blocks.keep_units(place_ref, (gate_kept, up_kept))
    hidden_rows(copies, rows_kept, gate_kept, up_kept, last_ref)
    downs.keep_down(down_kept)
    first_copy.wait()
    down_into(place_ref, (others_ref, mine_ref), first_kept, last_ref, down_kept)


def down_kernel(down_counts, place_ref, first_ref, last_ref, *refs):
    total = sum(down_counts)
    others_ref, mine_ref, first_kept, last_kept, staged, down_kept, sems, row_sems = refs[total:]
    downs = Staged(place_ref, grouped(refs[:total], down_counts), staged, sems)
    copies = [
        pltpu.make_async_copy(first_ref, first_kept, row_sems.at[0]),
        pltpu.make_async_copy(last_ref, last_kept, row_sems.at[1]),
    ]
    for copy in copies:
        copy.start()
    downs.keep_down(down_kept)
    for copy in copies:
        copy.wait()
    down_into(place_ref, (others_ref, mine_ref), first_kept, last_kept, down_kept)


def whole(*shape):
    return pl.BlockSpec(shape, lambda: (0,) * len(shape))


def kernel_call(kernel, place, arrays, outs, scratch):
    return pl.pallas_call(
        kernel,
        out_shape=[jax.ShapeDtypeStruct(shape, jnp.bfloat16) for shape in outs],
        in_specs=[pl.BlockSpec(memory_space=pltpu.SMEM)]
        + [pl.BlockSpec(memory_space=pltpu.HBM)] * len(arrays),
        out_specs=[whole(*shape) for shape in outs],
        scratch_shapes=scratch,
        compiler_params=pltpu.CompilerParams(vmem_limit_bytes=ALL_VMEM_BYTES),
        cost_estimate=pl.CostEstimate(flops=1000000, bytes_accessed=100000, transcendentals=0),
    )(place, *arrays)


def vmem(*shape):
    return pltpu.VMEM(shape, jnp.bfloat16)


def flat(sources):
    return [array for source in sources for array in source]


def early_hidden(place, rows, sources, own):
    units = (1 + len(sources) // 4) * UNITS
    scratch = [
        vmem(2 * ROWS, 2 * SPLIT),
        vmem(2, UNITS, 2 * SPLIT),
        vmem(len(sources), UNITS, SPLIT),
        vmem(units, 2 * SPLIT),
        vmem(units, 2 * SPLIT),
        pltpu.SemaphoreType.DMA((len(sources),)),
        pltpu.SemaphoreType.DMA((4,)),
    ]
    kernel = functools.partial(early_kernel, [len(source) for source in sources])
    return kernel_call(kernel, place, [rows, *flat(sources), *own], [(2 * ROWS, units)], scratch)[0]


def late_products(place, rows, first, sources, down_sources):
    scratch = [
        vmem(2 * ROWS, 2 * SPLIT),
        vmem(*first.shape),
        vmem(8, UNITS, SPLIT),
        vmem(UNITS, 2 * SPLIT),
        vmem(UNITS, 2 * SPLIT),
        vmem(4 * UNITS, SPLIT),
        pltpu.SemaphoreType.DMA((8,)),
        pltpu.SemaphoreType.DMA((3,)),
    ]
    kernel = functools.partial(late_kernel, [len(source) for source in sources], [len(source) for source in down_sources])
    arrays = [rows, first, *flat(sources), *flat(down_sources)]
    return kernel_call(kernel, place, arrays, [(ROWS, SPLIT), (ROWS, SPLIT), (2 * ROWS, UNITS)], scratch)


def down_products(place, first, last, down_sources):
    scratch = [
        vmem(*first.shape),
        vmem(*last.shape),
        vmem(4, UNITS, SPLIT),
        vmem(4 * UNITS, SPLIT),
        pltpu.SemaphoreType.DMA((4,)),
        pltpu.SemaphoreType.DMA((2,)),
    ]
    kernel = functools.partial(down_kernel, [len(source) for source in down_sources])
    return kernel_call(kernel, place, [first, last, *flat(down_sources)], [(ROWS, SPLIT)] * 2, scratch)


def spread_kernel(place_ref, places_ref, share_ref, *refs):
    out_ref = refs[-1]
    here = pl.multiple_of(place_ref[2] * SPLIT, SPLIT)
    places = places_ref[...]
    for index, lanes in enumerate((pl.ds(here, SPLIT), pl.ds(SPLIT - here, SPLIT))):
        if index == 0:
            picked = jnp.dot(places, refs[0][...], preferred_element_type=jnp.float32)
        else:
            expert_out = sum((ref[...].astype(jnp.float32) for ref in refs[2:5]), refs[1][...].astype(jnp.float32))
            high = expert_out.astype(jnp.bfloat16)
            low = (expert_out - high.astype(jnp.float32)).astype(jnp.bfloat16)
            picked = jnp.dot(
                jnp.concatenate([places, places], axis=1),
                jnp.concatenate([high, low], axis=0),
                preferred_element_type=jnp.float32,
            )
        out_ref[:, lanes] = (share_ref[...] * picked).astype(jnp.bfloat16)


def spread(place, places, share, pair, terms):
    def block(*shape):
        return pl.BlockSpec(shape, lambda i, place: (i, 0))

    slots = 2 * CAP
    own = pl.BlockSpec((slots, SPLIT), lambda i, place: (place[3] * (SPANS // 2) + i, 0))
    rows = block(slots, SPLIT)
    return pl.pallas_call(
        spread_kernel,
        out_shape=jax.ShapeDtypeStruct((SPANS * CT, 2 * SPLIT), jnp.bfloat16),
        grid_spec=pltpu.PrefetchScalarGridSpec(
            num_scalar_prefetch=1,
            grid=(SPANS // 2,),
            in_specs=[block(2 * CT, slots), block(2 * CT, 1), rows, own, own, rows, rows],
            out_specs=block(2 * CT, 2 * SPLIT),
        ),
        compiler_params=pltpu.CompilerParams(vmem_limit_bytes=ALL_VMEM_BYTES),
    )(place, places, share, terms[0], *pair, *terms[1:])


def on_device(tokens, expert_ids, gate_probs, gate_weight, up_weight, down_weight):
    model_width = tokens.shape[1]
    z_lo, y, core, x = (lax.axis_index(name) for name in ("z_lo", "y", "core", "x"))
    first = z_lo != core
    half = y % 2

    is_window = expert_ids == 0
    routed = jnp.any(is_window, axis=1)
    gate_share = jnp.sum(jnp.where(is_window, gate_probs, 0.0), axis=1)
    routed_blocks = routed.reshape(SPANS, CT)
    slot_place = jnp.cumsum(routed_blocks.astype(jnp.int32), axis=1) - 1
    selector = (
        slot_place[:, None, :] == jnp.arange(CAP, dtype=jnp.int32)[None, :, None]
    ) & routed_blocks[:, None, :]
    slot_rows = jnp.einsum(
        "bst,btd->bsd",
        selector.astype(jnp.bfloat16),
        tokens.reshape(SPANS, CT, model_width),
        preferred_element_type=jnp.float32,
    ).astype(jnp.bfloat16).reshape(SPANS * CAP, model_width)
    near_units, far_units = core * UNITS, (1 - core) * UNITS

    def piece(array, start, side):
        return lax.dynamic_slice(array, (start, side * SPLIT), (UNITS, SPLIT))

    shard = [gate_weight.T, up_weight.T, down_weight]
    order = [(0, near_units), (1, near_units), (2, near_units), (0, far_units), (1, far_units), (2, far_units)]
    own = [piece(shard[0], near_units, half)]
    place = jnp.stack([first.astype(jnp.int32), core, half, x])

    def joined(*parts):
        return jnp.concatenate(parts, axis=0)

    def pick(parts, index):
        return (parts[index], parts[index + 2])

    from_z, from_y = [], []
    work = slot_rows
    for step in range(13):
        if step < 5:
            feed = own[step]
        elif step < 7:
            feed = from_z[step - 3]
        elif step < 9:
            feed = own[5] if step == 7 else from_z[4]
        if step < 2:
            block = feed
        elif step < 9:
            block = jnp.where(first, feed, from_z[step - 2])
        else:
            block = from_z[step - 2]
        landed = max(step - 1, 0)
        settled = from_y[max(step - 4, 0) : max(step - 3, 0)]
        if step == 8:
            work["rows"] = rows
        block, from_z[:landed], settled, own, shard, work = lax.optimization_barrier(
            (block, from_z[:landed], settled, own, shard, work)
        )
        if step >= 4:
            from_y[step - 4] = settled[0]
        if step == 0:
            own.append(piece(shard[order[1][0]], order[1][1], half))
        if step == 1:
            own += [piece(shard[which], start, half) for which, start in order[2:]]
            work["own"] = [lax.dynamic_slice_in_dim(array, near_units, UNITS, 0) for array in shard[:2]]
            work["down"] = [own[2], piece(shard[2], near_units, 1 - half)]
            work["place"] = place
        if step < 11:
            from_z.append(moved(block, along_z))
        if step >= 2:
            from_y.append(moved(from_z[step - 2], along_y))
        if step == 0:
            rows = lax.all_gather(work, ("core", "x"), axis=0, tiled=True)
            work = {}
        def block_at(index):
            return [pick(from_z, index), pick(from_y, index), pick(from_z, index + 1), pick(from_y, index + 1)]

        if step == 10:
            work["hidden"] = early_hidden(work["place"], work["rows"], block_at(0) + block_at(3), work["own"])

    def downs(side, parts):
        return [(work["down"][side],), pick(parts, 2), pick(parts, 7), pick(parts, 8)]

    others_here, mine_here, last = late_products(work["place"], work["rows"], work["hidden"], block_at(5), downs(0, from_z))
    others_here, last, from_y[9], from_y[10] = lax.optimization_barrier((others_here, last, from_y[9], from_y[10]))
    sums_here = (mine_here.astype(jnp.float32) + moved(others_here, other_core).astype(jnp.float32)).astype(jnp.bfloat16)
    out_here = lax.psum_scatter(sums_here, "x", scatter_dimension=0, tiled=True)
    others_there, mine_there = down_products(work["place"], work["hidden"], last, downs(1, from_y))
    pair_there = (mine_there, moved(others_there, other_core))

    def summed(pair, step):
        start = (x + step) % 4 * (SPANS * CAP)
        first_part, second_part = (lax.dynamic_slice_in_dim(part, start, SPANS * CAP, 0) for part in pair)
        return first_part.astype(jnp.float32) + second_part.astype(jnp.float32)

    half_rows = SPANS * CAP // 2

    def far_pieces(pair):
        piece_on = summed(pair, 2).astype(jnp.bfloat16)
        return piece_on[:half_rows], piece_on[half_rows:]

    def far(pieces):
        return moved(pieces[0], along_x(1)), moved(pieces[1], along_x(3))

    def near(pair, arrived):
        above, below = summed(pair, 1), summed(pair, 3)
        above = joined(above[:half_rows] + arrived[0].astype(jnp.float32), above[half_rows:]).astype(jnp.bfloat16)
        below = joined(below[:half_rows], below[half_rows:] + arrived[1].astype(jnp.float32)).astype(jnp.bfloat16)
        return [moved(above, along_x(1)), moved(below, along_x(3))]

    pieces_there, pair_there = lax.optimization_barrier((far_pieces(pair_there), pair_there))
    near_there = near(pair_there, far(pieces_there))
    terms = [out_here, *near_there]
    pairs = jnp.swapaxes(selector, 1, 2).reshape(SPANS // 2, 2, CT, 1, CAP)
    pairs = pairs & jnp.eye(2, dtype=bool)[None, :, None, :, None]
    places = pairs.reshape(SPANS * CT, 2 * CAP).astype(jnp.bfloat16)
    return spread(work["place"], places, gate_share[:, None], pair_there, terms)


def solution(mesh):
    grid = Mesh(mesh.devices.reshape(SIZES), AXES)
    shard = ("z_hi", "x")
    in_specs = (
        P(AXES, None),
        P(AXES, None),
        P(AXES, None),
        P(None, shard),
        P(None, shard),
        P(shard, None),
    )
    return jax.shard_map(
        on_device, mesh=grid, in_specs=in_specs, out_specs=P(AXES, None), check_vma=False
    )
```
